32 devices in a mesh: groups: 2 (over y), mp: 4 (over z), segment: 2 (over x), section: 2 (over core).
Axes of the slice: x: 2, y: 2, z: 4, core: 2. Of those that a mesh axis runs over, the one named last changes fastest.
Arguments:
- resp_rows: bfloat16 [32, 32, 4096], P(('groups', 'segment'), None, 'mp'), parts along dimension 0, may hold values from -6 to 6
- lengths: int32 [8, 4], P('groups'), parts along dimension 0, may hold values from 1 to 32, 64 in all within a row
- source: int32 [32], P('groups'), parts along dimension 0, may hold values from 0 to 15, each once
- w_query: bfloat16 [2, 2, 4096, 1024], P('section', 'segment', None, 'mp'), may hold values from -0.09375 to 0.09375
- w_keyval: bfloat16 [2, 2, 4096, 2, 128], P('section', 'segment', None, None, 'mp'), may hold values from -0.09375 to 0.09375
- w_out: bfloat16 [2, 2, 1024, 4096], P('section', 'segment', None, 'mp'), may hold values from -0.1875 to 0.1875
- gains: bfloat16 [2, 2, 4096], P('section', 'segment', 'mp'), may hold values from 0.25 to 1.75
- final_gain: bfloat16 [2, 4096], P('section', 'mp'), may hold values from 0.25 to 1.75
- head: bfloat16 [2, 4096], P('section', 'mp'), may hold values from -0.09375 to 0.09375
Outputs:
- hidden: bfloat16 [2, 8, 64, 4096], P('section', 'groups', 'segment', 'mp'), parts along dimension 1
- scores: float32 [2, 8, 64], P('section', 'groups'), parts along dimension 1
- advantage: float32 [32], P(('groups', 'section')), parts along dimension 0
The draws below stay inside these ranges and needn't reach their ends.
There are 2 independent parts, one for each index of `groups`. The reference program is written for one: setup_inputs(seed, part) draws one part's arguments, and reference() takes and returns one part's arrays. A program takes and returns all parts, laid end to end along the dimension named above; an argument that names none is the same for every part. Nothing has to cross between parts.
Inputs may be any that keep to these rules, and one draw needn't show every extreme that they name: Each row of lengths sums to 64; its largest entry is exactly 32. source names every response once.
All inputs are finite; a program needn't handle non-finite values.
Results may differ from the reference program's by a relative error of at most 0.0085.
Values may be sent and summed in bfloat16 or wider, within the bound.
A program may use at most 64 MiB of HBM per device.

```python
import math
import jax
import jax.numpy as jnp
import numpy as np
from jax import lax

D = 4096
HEAD_DIM = 128
GROUP = 8
MB = 4
R_MB = 4
T_MB = 64
HEADS = 8
KV_HEADS = 1
LMAX = 32
RESP = 16
LAYERS = 2


def levels(own_key, extent, shards, low, top_value):
    level = 1.0
    for axis_at, parts in shards:
        heights = jax.random.uniform(jax.random.fold_in(jax.random.fold_in(own_key, 6), axis_at), (parts,), jnp.float32, low / len(shards), top_value / len(shards))
        level = level * jnp.repeat(jnp.exp(heights), extent[axis_at] // parts).reshape((-1,) + (1,) * (len(extent) - 1 - axis_at))
    return level


def length_profile(count, total, bound, lean):
    weights = [(1 << 20) // math.isqrt(rank ** lean) + 1 for rank in range(2, count + 1)]
    surplus, counts = total - bound - (count - 1), [1] * (count - 1)
    while surplus > 0:
        candidates = [i for i in range(count - 1) if counts[i] < bound]
        whole, left = sum([weights[i] for i in candidates]), surplus
        for i in candidates:
            addition = min(bound - counts[i], max(1, left * weights[i] // whole), surplus)
            counts[i] = counts[i] + addition
            surplus = surplus - addition
    return np.array([bound] + counts)


def uneven(stream_key, count, total, bound, skew):
    if count == 2:
        one = jax.random.randint(stream_key, (), max(1, total - bound), min(bound, total - 1) + 1)
        return jnp.stack([one, total - one])
    sizes = jnp.asarray(length_profile(count, total, bound, skew), jnp.int32)
    twos = (count - 1) // 2
    donor, sink = sizes[1:1 + 2 * twos:2], sizes[2:2 + 2 * twos:2]
    margin = jnp.minimum(donor - 1, bound - sink)
    passed = jax.random.randint(jax.random.fold_in(stream_key, 1), (twos,), 0, 1 << 20) % (margin + 1)
    sizes = sizes.at[1:1 + 2 * twos:2].set(donor - passed).at[2:2 + 2 * twos:2].set(sink + passed)
    return sizes[jax.random.permutation(jax.random.fold_in(stream_key, 2), count)]


def gaussian(rng, extent, deviation, bound, shards=(), held_as=jnp.bfloat16):
    loudness = levels(rng, extent, shards, -0.22, 0.18) if shards else 1.0
    array = jax.random.normal(rng, extent, jnp.float32) * deviation * loudness
    return jnp.minimum(jnp.maximum(array, -bound), bound).astype(held_as)


def setup_inputs(seed: int = 0, part: int = 0) -> dict:
    keys = jax.random.split(jax.random.key(seed), 10)
    own_keys = jax.random.split(jax.random.fold_in(keys[9], part), 10)
    return {
        "resp_rows": gaussian(own_keys[0], (RESP, LMAX, D), 1.0, 6.0, ((0, 2), (2, 4))),
        "lengths": jax.vmap(lambda own: uneven(own, R_MB, T_MB, LMAX, 2))(jax.random.split(own_keys[1], MB)).reshape((MB, R_MB)).astype(jnp.int32),
        "source": jax.random.permutation(own_keys[2], RESP).astype(jnp.int32),
        "w_query": gaussian(keys[3], (2, LAYERS, D, HEADS * HEAD_DIM), D ** -0.5, 0.09375, ((0, 2), (1, 2), (3, 4))),
        "w_keyval": gaussian(keys[4], (2, LAYERS, D, 2, KV_HEADS * HEAD_DIM), D ** -0.5, 0.09375, ((0, 2), (1, 2), (4, 4))),
        "w_out": gaussian(keys[5], (2, LAYERS, HEADS * HEAD_DIM, D), (HEADS * HEAD_DIM) ** -0.5, 0.1875, ((0, 2), (1, 2), (3, 4))),
        "gains": jnp.clip(1.0 + 0.15 * jax.random.normal(keys[6], (2, LAYERS, D), jnp.float32), 0.25, 1.75).astype(jnp.bfloat16),
        "final_gain": jnp.clip(1.0 + 0.15 * jax.random.normal(keys[7], (2, D), jnp.float32), 0.25, 1.75).astype(jnp.bfloat16),
        "head": gaussian(keys[8], (2, D), D ** -0.5, 0.09375, ((0, 2), (1, 4))),
    }


epsilon = 1e-06
rope_base = 1000000.0

def slot_tables(lengths, source):
    seg_ends = jnp.cumsum(lengths, axis=1).astype(jnp.int32)
    seg_starts = (seg_ends - lengths).astype(jnp.int32)
    places = jnp.arange(T_MB, dtype=jnp.int32)
    member = lax.optimization_barrier(jnp.sum((places[None, :, None] >= seg_ends[:, None, :]).astype(jnp.int32), axis=2)).astype(jnp.int32)
    one_hot = (member[:, :, None] == jnp.arange(R_MB, dtype=jnp.int32)[None, None, :]).astype(jnp.int32)
    position = (places[None, :] - lax.optimization_barrier(jnp.sum(one_hot * seg_starts[:, None, :], axis=2))).astype(jnp.int32)
    owners = lax.optimization_barrier(jnp.sum(one_hot * source.reshape(MB, R_MB)[:, None, :], axis=2)).astype(jnp.int32)
    return (member, position, owners, seg_ends)

def angles(position):
    inv_freqs = rope_base ** (-jnp.arange(0, HEAD_DIM // 2, dtype=jnp.float32) * 2.0 / HEAD_DIM)
    phases = position.astype(jnp.float32)[..., None] * inv_freqs
    return (jnp.cos(phases), jnp.sin(phases))

def rotate(vectors, cosine, sine_part):
    half_dim = vectors.shape[-1] // 2
    first_half = vectors[..., :half_dim]
    second_half = vectors[..., half_dim:]
    return jnp.concatenate([first_half * cosine - second_half * sine_part, second_half * cosine + first_half * sine_part], axis=-1)

def attention_layer(tok_rows, norm_gain, query_w, keyval_w, output_w, member, cosine, sine_part):
    rows_f32 = tok_rows.astype(jnp.float32)
    sq_sums = lax.optimization_barrier(jnp.sum(rows_f32 * rows_f32, axis=-1, keepdims=True))
    normed = (rows_f32 * lax.rsqrt(sq_sums / D + epsilon) * norm_gain.astype(jnp.float32)).astype(jnp.bfloat16)
    flat_rows = normed.reshape(MB * T_MB, D)
    queries = jnp.dot(flat_rows, query_w, preferred_element_type=jnp.float32).reshape(MB, T_MB, -1, HEAD_DIM)
    keyval = jnp.dot(flat_rows, keyval_w.reshape(D, -1), preferred_element_type=jnp.float32).astype(jnp.bfloat16)
    keyval = keyval.reshape(MB, T_MB, 2, -1, HEAD_DIM)
    cos_here = cosine[:, :, None, :]
    sin_here = sine_part[:, :, None, :]
    queries = rotate(queries, cos_here, sin_here).astype(jnp.bfloat16)
    key_rows = rotate(keyval[:, :, 0].astype(jnp.float32), cos_here, sin_here).astype(jnp.bfloat16)
    value_rows = keyval[:, :, 1]
    key_rows = jnp.repeat(key_rows, GROUP, axis=2)
    value_rows = jnp.repeat(value_rows, GROUP, axis=2)
    scores = jnp.einsum('bthd,bshd->bhts', queries.astype(jnp.float32), key_rows.astype(jnp.float32)) * HEAD_DIM ** (-0.5)
    places = jnp.arange(T_MB, dtype=jnp.int32)
    visible = (member[:, :, None] == member[:, None, :]) & (places[None, None, :] <= places[None, :, None])
    scores = jnp.where(visible[:, None], scores, jnp.float32(-1e+30))
    row_max = lax.optimization_barrier(jnp.max(scores, axis=-1, keepdims=True))
    expo = jnp.exp(scores - row_max)
    weights = (expo / lax.optimization_barrier(jnp.sum(expo, axis=-1, keepdims=True))).astype(jnp.bfloat16)
    attended = jnp.einsum('bhts,bshd->bthd', weights.astype(jnp.float32), value_rows.astype(jnp.float32)).astype(jnp.bfloat16)
    projected = jnp.dot(attended.reshape(MB * T_MB, -1), output_w, preferred_element_type=jnp.float32)
    return (rows_f32 + projected.reshape(MB, T_MB, D)).astype(jnp.bfloat16)

def reference(resp_rows, lengths, source, w_query, w_keyval, w_out, gains, final_gain, head):
    member, position, owners, seg_ends = slot_tables(lengths, source)
    cosine, sine_part = angles(position)
    packed = jnp.take(resp_rows.reshape(-1, D), (owners * LMAX + position).astype(jnp.int32), axis=0)
    hidden_list = []
    score_list = []
    for section_no in range(2):
        tok_rows = packed
        for layer_no in range(LAYERS):
            tok_rows = attention_layer(tok_rows, gains[section_no, layer_no], w_query[section_no, layer_no], w_keyval[section_no, layer_no], w_out[section_no, layer_no], member, cosine, sine_part)
        rows_f32 = tok_rows.astype(jnp.float32)
        sq_sums = lax.optimization_barrier(jnp.sum(rows_f32 * rows_f32, axis=-1, keepdims=True))
        normed = (rows_f32 * lax.rsqrt(sq_sums / D + epsilon) * final_gain[section_no].astype(jnp.float32)).astype(jnp.bfloat16)
        hidden_list.append(normed)
        score_list.append(lax.optimization_barrier(jnp.sum(normed.astype(jnp.float32) * head[section_no].astype(jnp.float32), axis=-1)))
    hidden = jnp.stack(hidden_list)
    scores = jnp.stack(score_list)
    places = jnp.arange(T_MB, dtype=jnp.int32)
    last_pick = (places[None, None, :] == (seg_ends - 1)[:, :, None]).astype(jnp.float32)
    slot_scores = lax.optimization_barrier(jnp.sum(last_pick[None] * scores[:, :, None, :], axis=-1))
    gap_slot = (slot_scores[0] - slot_scores[1]).reshape(-1)
    response_ids = jnp.arange(RESP, dtype=jnp.int32)
    matches = (source[None, :] == response_ids[:, None]).astype(jnp.float32)
    advantage = lax.optimization_barrier(jnp.sum(matches * gap_slot[None, :], axis=1))
    return (hidden, scores, advantage)
```

```python
import jax
import jax.numpy as jnp
from jax import lax
from jax.sharding import PartitionSpec as P

D = 4096
HEAD_DIM = 128
GROUP = 8
MB = 4
R_MB = 4
T_MB = 64
LMAX = 32
RESP = 16


epsilon = 1e-06
rope_base = 1000000.0


def from_partner(block, axis, stride):
    count = lax.axis_size(axis)
    route = []
    for low in range(count):
        high = low | 1 << stride
        if high != low and high < count:
            route += [(low, high), (high, low)]
    return lax.ppermute(block, axis, route)


def slot_tables(lengths, source):
    seg_ends = jnp.cumsum(lengths, axis=1)
    seg_starts = seg_ends - lengths
    places = jnp.arange(T_MB, dtype=jnp.int32)
    member = jnp.sum((places[None, :, None] >= seg_ends[:, None, :]).astype(jnp.int32), axis=2)
    one_hot = (member[:, :, None] == jnp.arange(R_MB, dtype=jnp.int32)[None, None, :]).astype(
        jnp.int32
    )
    position = places[None, :] - jnp.sum(one_hot * seg_starts[:, None, :], axis=2)
    owners = jnp.sum(one_hot * source.reshape(MB, R_MB)[:, None, :], axis=2)
    return (member, position, owners, seg_ends)


def angles(position):
    inv_freqs = rope_base ** (-jnp.arange(0, HEAD_DIM // 2, dtype=jnp.float32) * 2.0 / HEAD_DIM)
    phases = position.astype(jnp.float32)[..., None] * inv_freqs
    return (jnp.cos(phases), jnp.sin(phases))


def rotate(vectors, cosine, sine_part):
    half_dim = vectors.shape[-1] // 2
    first_half = vectors[..., :half_dim]
    second_half = vectors[..., half_dim:]
    return jnp.concatenate(
        [
            first_half * cosine - second_half * sine_part,
            second_half * cosine + first_half * sine_part,
        ],
        axis=-1,
    )


def layer(tok_rows, visible, cosine, sine_part, gain_all, query_w, keyval_w, output_w):
    width = tok_rows.shape[1]
    whole = lax.all_gather(tok_rows, "mp", axis=1, tiled=True)
    rows_f32 = whole.astype(jnp.float32)
    sq_sums = jnp.sum(rows_f32 * rows_f32, axis=1, keepdims=True)
    normed = (rows_f32 * lax.rsqrt(sq_sums / D + epsilon) * gain_all).astype(jnp.bfloat16)
    keyval = jnp.dot(normed, keyval_w, preferred_element_type=jnp.float32).astype(jnp.bfloat16)
    queries = jnp.dot(normed, query_w, preferred_element_type=jnp.float32)
    heads_here = query_w.shape[1] // HEAD_DIM
    kv_width = keyval_w.shape[1] // 2
    per_head = HEAD_DIM // kv_width
    all_keyval = lax.all_gather(keyval.reshape(MB, T_MB, 2, kv_width), "mp", axis=0)
    head_no = lax.axis_index("mp") * heads_here // GROUP
    chosen = lax.dynamic_slice_in_dim(all_keyval, head_no * per_head, per_head, 0)
    chosen = jnp.moveaxis(chosen, 0, 3).reshape(MB, T_MB, 2, HEAD_DIM)
    key_rows = rotate(chosen[:, :, 0].astype(jnp.float32), cosine, sine_part).astype(jnp.bfloat16)
    value_rows = chosen[:, :, 1]
    queries = rotate(
        queries.reshape(MB, T_MB, -1, HEAD_DIM), cosine[:, :, None, :], sine_part[:, :, None, :]
    ).astype(jnp.bfloat16)
    scores = jnp.einsum(
        "bthd,bsd->bhts", queries, key_rows, preferred_element_type=jnp.float32
    ) * HEAD_DIM ** (-0.5)
    scores = jnp.where(visible[:, None], scores, jnp.float32(-1e30))
    row_max = jnp.max(scores, axis=-1, keepdims=True)
    expo = jnp.exp(scores - row_max)
    weights = (expo / jnp.sum(expo, axis=-1, keepdims=True)).astype(jnp.bfloat16)
    attended = jnp.einsum(
        "bhts,bsd->bthd", weights, value_rows, preferred_element_type=jnp.float32
    ).astype(jnp.bfloat16)
    attended = attended.reshape(MB * T_MB, -1)
    projected = jnp.dot(
        lax.all_gather(attended, "mp", axis=1, tiled=True),
        output_w,
        preferred_element_type=jnp.float32,
    )
    return (tok_rows.astype(jnp.float32) + projected).astype(jnp.bfloat16)


def per_device(resp_rows, lengths, source, w_query, w_keyval, w_out, gains, final_gain, head):
    segment_count = lax.axis_size("segment")
    segment_no = lax.axis_index("segment")
    member, position, owners, seg_ends = slot_tables(lengths, source)
    cosine, sine_part = angles(position)
    places = jnp.arange(T_MB, dtype=jnp.int32)
    visible = (member[:, :, None] == member[:, None, :]) & (
        places[None, None, :] <= places[None, :, None]
    )
    gathered = lax.all_gather(resp_rows, "segment", axis=0, tiled=True)
    width = gathered.shape[2]
    x = jnp.take(gathered.reshape(-1, width), (owners * LMAX + position).reshape(-1), axis=0)
    gain_all = lax.all_gather(gains[0, 0], "mp", axis=0, tiled=True).astype(jnp.float32)
    query_w = w_query[0, 0]
    keyval_w = w_keyval[0, 0].reshape(D, -1)
    output_w = w_out[0, 0]
    for step in range(segment_count):
        y = layer(x, visible, cosine, sine_part, gain_all, query_w, keyval_w, output_w)
        if step < segment_count - 1:
            x = lax.ppermute(y, "segment", [(step, step + 1)])
    last = segment_count - 1
    rows_here = T_MB // segment_count
    y = y.reshape(MB, T_MB, width)
    blocks = [y[:, i * rows_here : (i + 1) * rows_here] for i in range(segment_count)]
    mine = blocks[last]
    for i in range(last):
        came = lax.ppermute(blocks[i], "segment", [(last, i)])
        mine = jnp.where(segment_no == i, came, mine)
    rows_f32 = mine.astype(jnp.float32)
    lift = final_gain[0].astype(jnp.float32)
    sums = jnp.stack(
        [jnp.sum(rows_f32 * rows_f32, axis=-1), jnp.sum(rows_f32 * (lift * head[0].astype(jnp.float32)), axis=-1)]
    )
    sums = jnp.sum(lax.all_gather(sums, "mp", axis=0), axis=0)
    scale = lax.rsqrt(sums[0] / D + epsilon)
    hidden = (rows_f32 * scale[..., None] * lift).astype(jnp.bfloat16)[None]
    scores = lax.all_gather(sums[1] * scale, "segment", axis=1, tiled=True)
    last_pick = (places[None, None, :] == (seg_ends - 1)[:, :, None]).astype(jnp.float32)
    slot_scores = jnp.sum(last_pick * scores[:, None, :], axis=-1)
    other_side = from_partner(slot_scores, "section", 0)
    section_no = lax.axis_index("section")
    gap_slot = jnp.where(section_no == 0, slot_scores - other_side, other_side - slot_scores).reshape(-1)
    half_count = RESP // 2
    response_ids = section_no * half_count + jnp.arange(half_count, dtype=jnp.int32)
    matches = (source[None, :] == response_ids[:, None]).astype(jnp.float32)
    own_part = jnp.sum(matches * gap_slot[None, :], axis=1)
    return (hidden, scores[None], own_part)


def solution(mesh):
    in_specs = (
        P(("groups", "segment"), None, "mp"),
        P("groups", None),
        P("groups"),
        P("section", "segment", None, "mp"),
        P("section", "segment", None, None, "mp"),
        P("section", "segment", None, "mp"),
        P("section", "segment", "mp"),
        P("section", "mp"),
        P("section", "mp"),
    )
    out_specs = (
        P("section", "groups", "segment", "mp"),
        P("section", "groups", None),
        P(("groups", "section")),
    )
    return jax.shard_map(
        per_device, mesh=mesh, in_specs=in_specs, out_specs=out_specs, check_vma=False
    )
```

```python
import functools

import jax
import jax.numpy as jnp
from jax import lax
from jax.experimental import pallas as pl
from jax.experimental.pallas import tpu as pltpu
from jax.sharding import PartitionSpec as P

D = 4096
HEAD_DIM = 128
GROUP = 8
MB = 4
R_MB = 4
T_MB = 64
LMAX = 32
RESP = 16


epsilon = 1e-06
rope_base = 1000000.0


def slot_tables(lengths, source):
    seg_ends = jnp.cumsum(lengths, axis=1)
    seg_starts = seg_ends - lengths
    places = jnp.arange(T_MB, dtype=jnp.int32)
    member = jnp.sum((places[None, :, None] >= seg_ends[:, None, :]).astype(jnp.int32), axis=2)
    one_hot = (member[:, :, None] == jnp.arange(R_MB, dtype=jnp.int32)[None, None, :]).astype(
        jnp.int32
    )
    position = places[None, :] - jnp.sum(one_hot * seg_starts[:, None, :], axis=2)
    owners = jnp.sum(one_hot * source.reshape(MB, R_MB)[:, None, :], axis=2)
    return (member, position, owners, seg_ends)


def angles(position):
    inv_freqs = rope_base ** (-jnp.arange(0, HEAD_DIM // 2, dtype=jnp.float32) * 2.0 / HEAD_DIM)
    phases = position.astype(jnp.float32)[..., None] * inv_freqs
    return (jnp.cos(phases), jnp.sin(phases))


def spin(block, cosine, signed_sine):
    return block * cosine + pltpu.roll(block, HEAD_DIM // 2, 1) * signed_sine


def stack_kernel(
    mp_count,
    seg_count,
    kv_width,
    resp,
    pick,
    code_col,
    base_col,
    code_row,
    cosine,
    signed_sine,
    gain,
    w_in,
    w_out,
    lift,
    lift_head,
    hidden,
    scores,
    other_scores,
    pool,
    x_own,
    x_all,
    gain_all,
    w_part,
    w_own,
    w_proj,
    part_out,
    part_in,
    acc,
    kv_all,
    att,
    y,
    y_in,
    stats,
    total,
    total_other,
    local_sem,
    pool_sem,
    gain_sem,
    half_sem,
    swap_sem,
    w_sem,
    part_sem,
    kv_sem,
    att_sem,
    next_sem,
    block_sem,
    stats_sem,
    total_sem,
    other_sem,
):
    f32, bf16 = jnp.float32, jnp.bfloat16
    me = lax.axis_index("mp")
    seg = lax.axis_index("segment")
    core = lax.axis_index("section")
    tokens, width = x_own.shape
    in_width = acc.shape[1]
    q_width = att.shape[1] // mp_count
    rows_pool = resp.shape[0]
    half = tokens // 2
    block = tokens // seg_count
    last = seg_count - 1
    group = HEAD_DIM // kv_width

    def peer(d):
        return lax.rem(me + d, mp_count)

    def source_of(d):
        return lax.rem(me + mp_count - d, mp_count)

    def remote(src, dst, sems, slot, **place):
        return pltpu.make_async_remote_copy(
            src_ref=src,
            dst_ref=dst,
            send_sem=sems.at[0, slot],
            recv_sem=sems.at[1, slot],
            device_id=place,
            device_id_type=pl.DeviceIdType.MESH,
        )

    barrier = pltpu.get_barrier_semaphore()
    for d in range(1, mp_count):
        pl.semaphore_signal(
            barrier, inc=1, device_id={"mp": peer(d)}, device_id_type=pl.DeviceIdType.MESH
        )
    for d in range(1, seg_count):
        pl.semaphore_signal(
            barrier,
            inc=1,
            device_id={"segment": lax.rem(seg + d, seg_count)},
            device_id_type=pl.DeviceIdType.MESH,
        )
    pl.semaphore_signal(
        barrier, inc=1, device_id={"section": 1 - core}, device_id_type=pl.DeviceIdType.MESH
    )
    proj_copy = pltpu.make_async_copy(w_out, w_proj, local_sem.at[0])
    proj_copy.start()
    pl.semaphore_wait(barrier, mp_count + seg_count - 1)

    def rows_of(index):
        return pl.ds(pl.multiple_of(index * width, width), width)

    lanes = lax.broadcasted_iota(jnp.int32, (tokens, in_width), 1)
    ss_lane = q_width + 2 * kv_width
    my_half = pl.ds(pl.multiple_of(core * half, half), half)
    its_half = pl.ds(pl.multiple_of((1 - core) * half, half), half)

    @pl.when(seg == 0)
    def _():
        own_w = pltpu.make_async_copy(w_in, w_own, local_sem.at[1])
        own_w.start()
        own_rows = pltpu.make_async_copy(resp, pool.at[0], local_sem.at[2])
        own_rows.start()
        gain_all[me] = gain[...]
        gain_copies = [
            remote(gain, gain_all.at[me], gain_sem, d, mp=peer(d)) for d in range(1, mp_count)
        ]
        for copy in gain_copies:
            copy.start()
        own_rows.wait()
        for s in range(1, seg_count):
            remote(resp, pool.at[s], pool_sem, s, segment=0).wait_recv()
        row_ids = lax.broadcasted_iota(jnp.int32, (tokens, rows_pool), 1)
        chosen = [
            (pick[...] - s * rows_pool == row_ids).astype(f32).astype(bf16) for s in range(seg_count)
        ]
        step = 256
        for at in range(0, width, step):
            found = jnp.dot(chosen[0], pool[0, :, at : at + step], preferred_element_type=f32)
            for s in range(1, seg_count):
                found += jnp.dot(chosen[s], pool[s, :, at : at + step], preferred_element_type=f32)
            x_own[:, at : at + step] = found.astype(bf16)
        halves = [
            remote(x_own.at[my_half], x_all.at[me, my_half], half_sem, d, mp=peer(d))
            for d in range(1, mp_count)
        ]
        for copy in halves:
            copy.start()
        own_w.wait()

        def shard(values, gains_row, index):
            rows = values.astype(f32)
            squares = jnp.sum(rows * rows, axis=1, keepdims=True)
            lifted = (rows * gains_row.astype(f32)).astype(bf16)
            product = jnp.dot(lifted, w_own[rows_of(index)], preferred_element_type=f32)
            return product + jnp.where(lanes == ss_lane, squares, 0.0)

        acc[...] = shard(x_own[...], gain[0:1], me)
        swaps = []
        for d in range(1, mp_count):
            halves[d - 1].wait_recv()
            here = x_all.at[source_of(d), my_half]
            swaps.append(remote(here, here, swap_sem, d, section=1 - core))
            swaps[-1].start()
        for d in range(1, mp_count):
            swaps[d - 1].wait_recv()
            gain_copies[d - 1].wait_recv()
            index = source_of(d)
            acc[...] += shard(x_all[index], gain_all[index, 0:1], index)
        for copy in halves + swaps + gain_copies:
            copy.wait_send()

    @pl.when(seg > 0)
    def _():
        rows_copy = remote(resp, pool.at[seg], pool_sem, seg, segment=0)
        rows_copy.start()
        own_w = pltpu.make_async_copy(w_in.at[rows_of(me)], w_part.at[me], local_sem.at[1])
        own_w.start()
        w_copies = [
            remote(w_in.at[rows_of(peer(d))], w_part.at[me], w_sem, d, mp=peer(d))
            for d in range(1, mp_count)
        ]
        for copy in w_copies:
            copy.start()
        own_w.wait()
        rows_copy.wait_send()
        for copy in w_copies:
            copy.wait()
        remote(y, x_own, next_sem, 0, segment=lax.rem(seg + 1, seg_count)).wait_recv()
        rows = x_own[...].astype(f32)
        squares = jnp.sum(rows * rows, axis=1, keepdims=True)
        upper = squares.astype(bf16).astype(f32)
        lower = squares - upper
        lifted = (rows * gain[0:1].astype(f32)).astype(bf16)
        extra = jnp.where(lanes == ss_lane, upper, jnp.where(lanes == ss_lane + 1, lower, 0.0))
        copies = []
        for d in range(1, mp_count):
            product = jnp.dot(lifted, w_part[peer(d)], preferred_element_type=f32)
            part_out[d] = (product + extra).astype(bf16)
            copies.append(remote(part_out.at[d], part_in.at[d], part_sem, d, mp=peer(d)))
            copies[-1].start()
        acc[...] = jnp.dot(lifted, w_part[me], preferred_element_type=f32) + extra
        for d in range(1, mp_count):
            copies[d - 1].wait_recv()
            acc[...] += part_in[d].astype(f32)
        for copy in copies:
            copy.wait_send()

    squares = acc[:, ss_lane : ss_lane + 1] + acc[:, ss_lane + 1 : ss_lane + 2]
    scale = lax.rsqrt(squares / D + epsilon)
    slot = lax.rem(me, group)
    kv_all[slot] = (acc[:, q_width:] * scale).astype(bf16)
    kv_copies = [
        remote(
            kv_all.at[slot], kv_all.at[slot], kv_sem, d, mp=me - slot + lax.rem(slot + d, group)
        )
        for d in range(1, group)
    ]
    for copy in kv_copies:
        copy.start()
    cos_here, sin_here = cosine[...], signed_sine[...]
    head_count = q_width // HEAD_DIM
    queries = []
    for h in range(head_count):
        vectors = acc[:, h * HEAD_DIM : (h + 1) * HEAD_DIM] * scale
        queries.append(spin(vectors, cos_here, sin_here).astype(bf16))
    codes = code_row[...]
    visible = (codes <= code_col[...]) & (codes >= base_col[...])
    for copy in kv_copies:
        copy.wait()
    kv_lanes = kv_all.shape[2]
    from_lane = lax.broadcasted_iota(jnp.int32, (kv_lanes, 2 * HEAD_DIM), 0)
    to_lane = lax.broadcasted_iota(jnp.int32, (kv_lanes, 2 * HEAD_DIM), 1)
    keyval = jnp.zeros((tokens, 2 * HEAD_DIM), f32)
    for g in range(group):
        place = jnp.where(
            from_lane < kv_width,
            from_lane + g * kv_width,
            from_lane - kv_width + HEAD_DIM + g * kv_width,
        )
        moved = (place == to_lane) & (from_lane < 2 * kv_width)
        keyval += jnp.dot(kv_all[g], moved.astype(f32).astype(bf16), preferred_element_type=f32)
    key_rows = spin(keyval[:, :HEAD_DIM], cos_here, sin_here).astype(bf16)
    value_rows = keyval[:, HEAD_DIM:].astype(bf16)
    outs = []
    for h in range(head_count):
        logits = lax.dot_general(
            queries[h], key_rows, (((1,), (1,)), ((), ())), preferred_element_type=f32
        ) * HEAD_DIM ** (-0.5)
        logits = jnp.where(visible, logits, -1e30)
        expo = jnp.exp(logits - jnp.max(logits, axis=1, keepdims=True))
        weights = (expo / jnp.sum(expo, axis=1, keepdims=True)).astype(bf16)
        outs.append(jnp.dot(weights, value_rows, preferred_element_type=f32).astype(bf16))
    my_columns = pl.ds(pl.multiple_of(me * q_width, q_width), q_width)
    att[:, my_columns] = jnp.concatenate(outs, axis=1)
    att_copies = [
        remote(att.at[:, my_columns], att.at[:, my_columns], att_sem, d, mp=peer(d))
        for d in range(1, mp_count)
    ]
    for copy in att_copies:
        copy.start()
    proj_copy.wait()
    for copy in att_copies:
        copy.wait()
    step = 256
    for at in range(0, width, step):
        projected = jnp.dot(att[...], w_proj[:, at : at + step], preferred_element_type=f32)
        y[:, at : at + step] = (x_own[:, at : at + step].astype(f32) + projected).astype(bf16)

    @pl.when(seg < last)
    def _():
        onward = remote(y, x_own, next_sem, 0, segment=lax.rem(seg + 1, seg_count))
        onward.start()
        onward.wait_send()
        remote(y.at[pl.ds(0, block)], y_in, block_sem, seg, segment=0).wait_recv()
        remote(total, total, total_sem, seg, segment=0).wait_recv()

    @pl.when(seg == last)
    def _():
        blocks = [
            remote(y.at[pl.ds(i * block, block)], y_in, block_sem, i, segment=i)
            for i in range(last)
        ]
        for copy in blocks:
            copy.start()
        rows = y[...].astype(f32)
        squares = jnp.sum(rows * rows, axis=1, keepdims=True)
        dots = jnp.sum(rows * lift_head[...], axis=1, keepdims=True)
        lane = lax.broadcasted_iota(jnp.int32, (tokens, HEAD_DIM), 1)
        both = jnp.where(lane == 0, squares, jnp.where(lane == 1, dots, 0.0))
        stats[0] = jnp.transpose(both)[:8]
        copies = [
            remote(stats.at[0], stats.at[d], stats_sem, d, mp=peer(d)) for d in range(1, mp_count)
        ]
        for copy in copies:
            copy.start()
        for copy in copies:
            copy.wait()
        total[...] = jnp.sum(stats[...], axis=0)
        totals = [remote(total, total, total_sem, i, segment=i) for i in range(last)]
        for copy in totals:
            copy.start()
        for copy in blocks + totals:
            copy.wait_send()
        y_in[...] = y[last * block : (last + 1) * block]

    swap = remote(total, total_other, other_sem, 0, section=1 - core)
    swap.start()
    row_scale = lax.rsqrt(total[0:1] / D + epsilon)
    scores[...] = jnp.broadcast_to(total[1:2] * row_scale, scores.shape)
    at_token = lax.broadcasted_iota(jnp.int32, (block, tokens), 1)
    wanted = lax.broadcasted_iota(jnp.int32, (block, tokens), 0) + seg * block
    column = jnp.sum(jnp.where(at_token == wanted, row_scale, 0.0), axis=1, keepdims=True)
    hidden[...] = (y_in[...].astype(f32) * column * lift[...]).astype(bf16)
    swap.wait()
    other_scores[...] = jnp.broadcast_to(
        total_other[1:2] * lax.rsqrt(total_other[0:1] / D + epsilon), other_scores.shape
    )


def per_device(resp_rows, lengths, source, w_query, w_keyval, w_out, gains, final_gain, head):
    seg_count = lax.axis_size("segment")
    mp_count = lax.axis_size("mp")
    f32, bf16 = jnp.float32, jnp.bfloat16
    member, position, owners, seg_ends = slot_tables(lengths, source)
    width = resp_rows.shape[2]
    rows_here = T_MB // seg_count
    tokens = MB * T_MB
    block = tokens // seg_count

    def ordered(table):
        return table.reshape(MB, seg_count, rows_here).transpose(1, 0, 2).reshape(-1)

    slots = ordered(member + R_MB * jnp.arange(MB, dtype=jnp.int32)[:, None])
    spots = ordered(position)
    pick = ordered(owners) * LMAX + spots
    base = slots * T_MB
    code = base + spots
    cosine, sine_part = angles(spots)
    cosine = jnp.concatenate([cosine, cosine], axis=1)
    signed_sine = jnp.concatenate([-sine_part, sine_part], axis=1)
    kv_width = w_keyval.shape[-1]
    q_width = w_query.shape[-1]
    kv_lanes = HEAD_DIM
    keyval_w = w_keyval[0, 0].reshape(D, 2 * kv_width)
    w_in = jnp.concatenate(
        [w_query[0, 0], keyval_w, jnp.zeros((D, kv_lanes - 2 * kv_width), bf16)], axis=1
    )
    in_width = q_width + kv_lanes
    lift = final_gain.astype(f32)
    rows_pool = resp_rows.shape[0] * LMAX
    vmem = pl.BlockSpec(memory_space=pltpu.VMEM)
    hbm = pl.BlockSpec(memory_space=pl.ANY)
    group = HEAD_DIM // kv_width
    dma = pltpu.SemaphoreType.DMA
    hidden, scores, other = pl.pallas_call(
        functools.partial(stack_kernel, mp_count, seg_count, kv_width),
        out_shape=(
            jax.ShapeDtypeStruct((block, width), bf16),
            jax.ShapeDtypeStruct((8, tokens), f32),
            jax.ShapeDtypeStruct((8, tokens), f32),
        ),
        in_specs=[hbm, vmem, vmem, vmem, vmem, vmem, vmem, vmem, hbm, hbm, vmem, vmem],
        out_specs=(vmem, vmem, vmem),
        scratch_shapes=[
            pltpu.VMEM((seg_count, rows_pool, width), bf16),
            pltpu.VMEM((tokens, width), bf16),
            pltpu.VMEM((mp_count, tokens, width), bf16),
            pltpu.VMEM((mp_count, 16, width), bf16),
            pltpu.VMEM((mp_count, width, in_width), bf16),
            pltpu.VMEM((D, in_width), bf16),
            pltpu.VMEM((mp_count * q_width, width), bf16),
            pltpu.VMEM((mp_count, tokens, in_width), bf16),
            pltpu.VMEM((mp_count, tokens, in_width), bf16),
            pltpu.VMEM((tokens, in_width), f32),
            pltpu.VMEM((group, tokens, kv_lanes), bf16),
            pltpu.VMEM((tokens, mp_count * q_width), bf16),
            pltpu.VMEM((tokens, width), bf16),
            pltpu.VMEM((block, width), bf16),
            pltpu.VMEM((mp_count, 8, tokens), f32),
            pltpu.VMEM((8, tokens), f32),
            pltpu.VMEM((8, tokens), f32),
            dma((3,)),
            dma((2, seg_count)),
            dma((2, mp_count)),
            dma((2, mp_count)),
            dma((2, mp_count)),
            dma((2, mp_count)),
            dma((2, mp_count)),
            dma((2, group)),
            dma((2, mp_count)),
            dma((2, 1)),
            dma((2, seg_count)),
            dma((2, mp_count)),
            dma((2, seg_count)),
            dma((2, 1)),
        ],
        compiler_params=pltpu.CompilerParams(
            collective_id=0, has_side_effects=True, vmem_limit_bytes=44 * 1024 * 1024
        ),
    )(
        resp_rows.reshape(rows_pool, width),
        pick[:, None],
        code[:, None],
        base[:, None],
        code[None, :],
        cosine,
        signed_sine,
        jnp.broadcast_to(gains[0], (16, width)),
        w_in,
        w_out[0, 0],
        lift,
        lift * head.astype(f32),
    )

    def restored(row):
        return row.reshape(seg_count, MB, rows_here).transpose(1, 0, 2).reshape(MB, T_MB)

    scores, other = restored(scores[0]), restored(other[0])
    hidden = hidden.reshape(1, MB, rows_here, width)
    places = jnp.arange(T_MB, dtype=jnp.int32)
    last_pick = (places[None, None, :] == (seg_ends - 1)[:, :, None]).astype(f32)
    section_no = lax.axis_index("section")
    gap = jnp.where(section_no == 0, scores - other, other - scores)
    gap_slot = jnp.sum(last_pick * gap[:, None, :], axis=-1).reshape(-1)
    half_count = RESP // 2
    response_ids = section_no * half_count + jnp.arange(half_count, dtype=jnp.int32)
    matches = (source[None, :] == response_ids[:, None]).astype(f32)
    own_part = jnp.sum(matches * gap_slot[None, :], axis=1)
    return (hidden, scores[None], own_part)


def solution(mesh):
    in_specs = (
        P(("groups", "segment"), None, "mp"),
        P("groups", None),
        P("groups"),
        P("section", "segment", None, "mp"),
        P("section", "segment", None, None, "mp"),
        P("section", "segment", None, "mp"),
        P("section", "segment", "mp"),
        P("section", "mp"),
        P("section", "mp"),
    )
    out_specs = (
        P("section", "groups", "segment", "mp"),
        P("section", "groups", None),
        P(("groups", "section")),
    )
    return jax.shard_map(
        per_device, mesh=mesh, in_specs=in_specs, out_specs=out_specs, check_vma=False
    )
```

```python
import functools

import jax
import jax.numpy as jnp
from jax import lax
from jax.experimental import pallas as pl
from jax.experimental.pallas import tpu as pltpu
from jax.sharding import PartitionSpec as P

D = 4096
HEAD_DIM = 128
GROUP = 8
MB = 4
R_MB = 4
T_MB = 64
LMAX = 32
RESP = 16


epsilon = 1e-06
rope_base = 1000000.0


def slot_tables(lengths, source):
    seg_ends = jnp.cumsum(lengths, axis=1)
    seg_starts = seg_ends - lengths
    places = jnp.arange(T_MB, dtype=jnp.int32)
    member = jnp.sum((places[None, :, None] >= seg_ends[:, None, :]).astype(jnp.int32), axis=2)
    one_hot = (member[:, :, None] == jnp.arange(R_MB, dtype=jnp.int32)[None, None, :]).astype(
        jnp.int32
    )
    position = places[None, :] - jnp.sum(one_hot * seg_starts[:, None, :], axis=2)
    owners = jnp.sum(one_hot * source.reshape(MB, R_MB)[:, None, :], axis=2)
    return (member, position, owners, seg_ends)


def angles(position):
    inv_freqs = rope_base ** (-jnp.arange(0, HEAD_DIM // 2, dtype=jnp.float32) * 2.0 / HEAD_DIM)
    phases = position.astype(jnp.float32)[..., None] * inv_freqs
    return (jnp.cos(phases), jnp.sin(phases))


def spin(block, cosine, signed_sine):
    return block * cosine + pltpu.roll(block, HEAD_DIM // 2, 1) * signed_sine


def stack_kernel(
    mp_count,
    seg_count,
    kv_width,
    resp,
    pick,
    code_col,
    code_row,
    cosine,
    signed_sine,
    gain,
    w_query,
    w_keyval,
    w_out,
    final_gain,
    head,
    hidden,
    scores,
    other_scores,
    pool,
    x_own,
    x_all,
    gain_all,
    query_part,
    keyval_part,
    query_own,
    keyval_own,
    w_proj,
    part_out,
    part_in,
    acc,
    kv_all,
    att,
    y,
    y_in,
    stats,
    total,
    total_other,
    local_sem,
    pool_sem,
    gain_sem,
    half_sem,
    swap_sem,
    w_sem,
    share_sem,
    part_sem,
    kv_sem,
    att_sem,
    next_sem,
    block_sem,
    stats_sem,
    total_sem,
    other_sem,
):
    f32, bf16 = jnp.float32, jnp.bfloat16
    me = lax.axis_index("mp")
    seg = lax.axis_index("segment")
    core = lax.axis_index("section")
    team = lax.axis_index("groups")
    tokens, width = x_own.shape
    in_width = acc.shape[1]
    q_width = att.shape[1] // mp_count
    rows_pool = resp.shape[0]
    half = tokens // 2
    half_width = width // 2
    block = tokens // seg_count
    last = seg_count - 1
    group = HEAD_DIM // kv_width

    def peer(d):
        return lax.rem(me + d, mp_count)

    def source_of(d):
        return lax.rem(me + mp_count - d, mp_count)

    def remote(src, dst, sems, slot, **place):
        return pltpu.make_async_remote_copy(
            src_ref=src,
            dst_ref=dst,
            send_sem=sems.at[0, slot],
            recv_sem=sems.at[1, slot],
            device_id=place,
            device_id_type=pl.DeviceIdType.MESH,
        )

    barrier = pltpu.get_barrier_semaphore()
    for d in range(1, mp_count):
        pl.semaphore_signal(
            barrier, inc=1, device_id={"mp": peer(d)}, device_id_type=pl.DeviceIdType.MESH
        )
    for d in range(1, seg_count):
        pl.semaphore_signal(
            barrier,
            inc=1,
            device_id={"segment": lax.rem(seg + d, seg_count)},
            device_id_type=pl.DeviceIdType.MESH,
        )
    pl.semaphore_signal(
        barrier, inc=1, device_id={"section": 1 - core}, device_id_type=pl.DeviceIdType.MESH
    )
    pl.semaphore_signal(
        barrier, inc=1, device_id={"groups": 1 - team}, device_id_type=pl.DeviceIdType.MESH
    )
    proj_copy = pltpu.make_async_copy(w_out, w_proj, local_sem.at[0])
    proj_copy.start()
    pl.semaphore_wait(barrier, mp_count + seg_count)

    def rows_of(index):
        return pl.ds(pl.multiple_of(index * width, width), width)

    ss_lane = q_width + 2 * kv_width
    kv_lanes = in_width - q_width
    my_columns = pl.ds(pl.multiple_of(core * half_width, half_width), half_width)

    @pl.when(seg == 0)
    def _():
        own_rows = pltpu.make_async_copy(resp.at[:, my_columns], pool.at[0], local_sem.at[3])
        own_rows.start()
        own_query = pltpu.make_async_copy(w_query, query_own, local_sem.at[1])
        own_query.start()
        own_keyval = pltpu.make_async_copy(w_keyval, keyval_own, local_sem.at[2])
        own_keyval.start()
        gain_all[me] = gain[...]
        gain_copies = [
            remote(gain, gain_all.at[me], gain_sem, d, mp=peer(d)) for d in range(1, mp_count)
        ]
        for copy in gain_copies:
            copy.start()
        row_ids = lax.broadcasted_iota(jnp.int32, (tokens, rows_pool), 1)
        chosen = [
            (pick[...] - s * rows_pool == row_ids).astype(f32).astype(bf16) for s in range(seg_count)
        ]
        own_rows.wait()
        for s in range(1, seg_count):
            remote(resp.at[:, my_columns], pool.at[s], pool_sem, s, segment=0).wait_recv()
        step = min(256, half_width)
        for at in range(0, half_width, step):
            found = jnp.dot(chosen[0], pool[0, :, at : at + step], preferred_element_type=f32)
            for s in range(1, seg_count):
                found += jnp.dot(chosen[s], pool[s, :, at : at + step], preferred_element_type=f32)
            x_own[:, pl.ds(pl.multiple_of(core * half_width + at, step), step)] = found.astype(bf16)
        packed = x_own.at[:, my_columns]
        halves = [
            remote(packed, x_all.at[me, :, my_columns], half_sem, d, mp=peer(d))
            for d in range(1, mp_count)
        ]
        for copy in halves:
            copy.start()
        swaps = [remote(packed, packed, swap_sem, 0, section=1 - core)]
        swaps[0].start()
        own_query.wait()
        own_keyval.wait()
        lane = lax.broadcasted_iota(jnp.int32, (tokens, kv_lanes), 1)

        def shard(values, gains_row, index):
            rows = values.astype(f32)
            squares = jnp.sum(rows * rows, axis=1, keepdims=True)
            lifted = (rows * gains_row.astype(f32)).astype(bf16)
            at = rows_of(index)
            acc[:, :q_width] += jnp.dot(lifted, query_own[at], preferred_element_type=f32)
            keyval = jnp.dot(lifted, keyval_own[at], preferred_element_type=f32)
            acc[:, q_width:] += keyval + jnp.where(lane == 2 * kv_width, squares, 0.0)

        def add(d):
            swaps[d].wait_recv()
            if d == 0:
                shard(x_own[...], gain[0:1], me)
            else:
                gain_copies[d - 1].wait_recv()
                index = source_of(d)
                shard(x_all[index], gain_all[index, 0:1], index)

        acc[...] = jnp.zeros_like(acc)
        for d in range(1, mp_count):
            here = x_all.at[source_of(d), :, my_columns]
            swaps.append(remote(here, here, swap_sem, d, section=1 - core))
        order = []
        for d in range(1, mp_count // 2 + 1):
            order += [d] if 2 * d == mp_count else [d, mp_count - d]
        done = 0
        for d in order:
            halves[d - 1].wait_recv()
            swaps[d].start()
            add(done)
            done = d
        add(done)
        for copy in halves + swaps + gain_copies:
            copy.wait_send()

    @pl.when(seg > 0)
    def _():
        rows_copy = remote(resp.at[:, my_columns], pool.at[seg], pool_sem, seg, segment=0)
        rows_copy.start()
        upper_rows = pl.ds(pl.multiple_of(team * half_width, half_width), half_width)
        weights = [(w_query, query_part), (w_keyval, keyval_part)]
        shards = []
        shares = []
        for i, (whole, part) in enumerate(weights):
            for d in range(1, mp_count):
                rows = pl.ds(
                    pl.multiple_of(peer(d) * width + team * half_width, half_width), half_width
                )
                here = part.at[source_of(d), upper_rows]
                slot = i * mp_count + d
                shards.append(
                    remote(whole.at[rows], part.at[me, upper_rows], w_sem, slot, mp=peer(d))
                )
                shares.append(remote(here, here, share_sem, slot, groups=1 - team))
        for copy in shards:
            copy.start()
        for i, (whole, part) in enumerate(weights):
            own = pltpu.make_async_copy(whole.at[rows_of(me)], part.at[me], local_sem.at[1 + i])
            own.start()
            own.wait()
        rows_copy.wait_send()
        for copy, share in zip(shards, shares):
            copy.wait_recv()
            share.start()
        for share in shares:
            share.wait()
        for copy in shards:
            copy.wait_send()
        lane = lax.broadcasted_iota(jnp.int32, (half, kv_lanes), 1)
        copies = []
        for r in range(2):
            mine = pl.ds(r * half, half)
            remote(
                y.at[mine], x_own.at[mine], next_sem, r, segment=lax.rem(seg + 1, seg_count)
            ).wait_recv()
            rows = x_own[mine].astype(f32)
            squares = jnp.sum(rows * rows, axis=1, keepdims=True)
            upper = squares.astype(bf16).astype(f32)
            extra = jnp.where(
                lane == 2 * kv_width,
                upper,
                jnp.where(lane == 2 * kv_width + 1, squares - upper, 0.0),
            )
            lifted = (rows * gain[0:1].astype(f32)).astype(bf16)
            for d in range(1, mp_count):
                index = peer(d)
                part_out[d, mine, :q_width] = jnp.dot(
                    lifted, query_part[index], preferred_element_type=f32
                ).astype(bf16)
                part_out[d, mine, q_width:] = (
                    jnp.dot(lifted, keyval_part[index], preferred_element_type=f32) + extra
                ).astype(bf16)
                copies.append(
                    remote(
                        part_out.at[d, mine],
                        part_in.at[d, mine],
                        part_sem,
                        r * mp_count + d,
                        mp=index,
                    )
                )
                copies[-1].start()
            acc[mine, :q_width] = jnp.dot(lifted, query_part[me], preferred_element_type=f32)
            acc[mine, q_width:] = (
                jnp.dot(lifted, keyval_part[me], preferred_element_type=f32) + extra
            )
        for r in range(2):
            mine = pl.ds(r * half, half)
            for d in range(1, mp_count):
                copies[r * (mp_count - 1) + d - 1].wait_recv()
                acc[mine] += part_in[d, mine].astype(f32)
        for copy in copies:
            copy.wait_send()

    squares = acc[:, ss_lane : ss_lane + 1] + acc[:, ss_lane + 1 : ss_lane + 2]
    scale = lax.rsqrt(squares / D + epsilon)
    slot = lax.rem(me, group)
    kv_all[slot] = (acc[:, q_width:] * scale).astype(bf16)
    kv_copies = [
        remote(
            kv_all.at[slot], kv_all.at[slot], kv_sem, d, mp=me - slot + lax.rem(slot + d, group)
        )
        for d in range(1, group)
    ]
    for copy in kv_copies:
        copy.start()
    cos_here, sin_here = cosine[...], signed_sine[...]
    head_count = q_width // HEAD_DIM
    queries = []
    for h in range(head_count):
        vectors = acc[:, h * HEAD_DIM : (h + 1) * HEAD_DIM] * scale
        queries.append(spin(vectors, cos_here, sin_here).astype(bf16))
    codes = code_row[...]
    visible = (codes <= code_col[...]) & (codes >= code_col[...] // T_MB * T_MB)
    for copy in kv_copies:
        copy.wait()
    from_lane = lax.broadcasted_iota(jnp.int32, (kv_lanes, 2 * HEAD_DIM), 0)
    to_lane = lax.broadcasted_iota(jnp.int32, (kv_lanes, 2 * HEAD_DIM), 1)
    keyval = jnp.zeros((tokens, 2 * HEAD_DIM), f32)
    for g in range(group):
        place = jnp.where(
            from_lane < kv_width,
            from_lane + g * kv_width,
            from_lane - kv_width + HEAD_DIM + g * kv_width,
        )
        moved = (place == to_lane) & (from_lane < 2 * kv_width)
        keyval += jnp.dot(kv_all[g], moved.astype(f32).astype(bf16), preferred_element_type=f32)
    key_rows = spin(keyval[:, :HEAD_DIM], cos_here, sin_here).astype(bf16)
    value_rows = keyval[:, HEAD_DIM:].astype(bf16)
    outs = []
    for h in range(head_count):
        logits = lax.dot_general(
            queries[h], key_rows, (((1,), (1,)), ((), ())), preferred_element_type=f32
        ) * HEAD_DIM ** (-0.5)
        logits = jnp.where(visible, logits, -1e30)
        expo = jnp.exp(logits - jnp.max(logits, axis=1, keepdims=True))
        weights = (expo / jnp.sum(expo, axis=1, keepdims=True)).astype(bf16)
        outs.append(jnp.dot(weights, value_rows, preferred_element_type=f32).astype(bf16))
    att_columns = pl.ds(pl.multiple_of(me * q_width, q_width), q_width)
    att[:, att_columns] = jnp.concatenate(outs, axis=1)
    att_copies = [
        remote(att.at[:, att_columns], att.at[:, att_columns], att_sem, d, mp=peer(d))
        for d in range(1, mp_count)
    ]
    for copy in att_copies:
        copy.start()
    proj_copy.wait()
    for copy in att_copies:
        copy.wait()
    step = 256

    def onward(r):
        mine = pl.ds(r * half, half)
        return remote(
            y.at[mine], x_own.at[mine], next_sem, r, segment=lax.rem(seg + 1, seg_count)
        )

    for r in range(2):
        mine = pl.ds(r * half, half)
        for at in range(0, width, step):
            projected = jnp.dot(
                att[mine], w_proj[:, at : at + step], preferred_element_type=f32
            )
            y[mine, at : at + step] = (
                x_own[mine, at : at + step].astype(f32) + projected
            ).astype(bf16)

        @pl.when(seg < last)
        def _():
            onward(r).start()

    lift = final_gain[...].astype(f32)
    lift_head = lift * head[...].astype(f32)

    @pl.when(seg < last)
    def _():
        for r in range(2):
            onward(r).wait_send()
        remote(y.at[pl.ds(0, block)], y_in, block_sem, seg, segment=0).wait_recv()
        remote(total, total, total_sem, seg, segment=0).wait_recv()

    @pl.when(seg == last)
    def _():
        blocks = [
            remote(y.at[pl.ds(i * block, block)], y_in, block_sem, i, segment=i)
            for i in range(last)
        ]
        for copy in blocks:
            copy.start()
        rows = y[...].astype(f32)
        squares = jnp.sum(rows * rows, axis=1, keepdims=True)
        dots = jnp.sum(rows * lift_head, axis=1, keepdims=True)
        lane = lax.broadcasted_iota(jnp.int32, (tokens, HEAD_DIM), 1)
        both = jnp.where(lane == 0, squares, jnp.where(lane == 1, dots, 0.0))
        stats[0] = jnp.transpose(both)[:8]
        copies = [
            remote(stats.at[0], stats.at[d], stats_sem, d, mp=peer(d)) for d in range(1, mp_count)
        ]
        for copy in copies:
            copy.start()
        for copy in copies:
            copy.wait()
        total[...] = jnp.sum(stats[...], axis=0)
        totals = [remote(total, total, total_sem, i, segment=i) for i in range(last)]
        for copy in totals:
            copy.start()
        for copy in blocks + totals:
            copy.wait_send()
        y_in[...] = y[last * block : (last + 1) * block]

    swap = remote(total, total_other, other_sem, 0, section=1 - core)
    swap.start()
    row_scale = lax.rsqrt(total[0:1] / D + epsilon)
    scores[...] = jnp.broadcast_to(total[1:2] * row_scale, scores.shape)
    at_token = lax.broadcasted_iota(jnp.int32, (block, tokens), 1)
    wanted = lax.broadcasted_iota(jnp.int32, (block, tokens), 0) + seg * block
    column = jnp.sum(jnp.where(at_token == wanted, row_scale, 0.0), axis=1, keepdims=True)
    hidden[...] = (y_in[...].astype(f32) * column * lift).astype(bf16)
    swap.wait()
    other_scores[...] = jnp.broadcast_to(
        total_other[1:2] * lax.rsqrt(total_other[0:1] / D + epsilon), other_scores.shape
    )


def per_device(resp_rows, lengths, source, w_query, w_keyval, w_out, gains, final_gain, head):
    seg_count = lax.axis_size("segment")
    mp_count = lax.axis_size("mp")
    f32, bf16 = jnp.float32, jnp.bfloat16
    member, position, owners, seg_ends = slot_tables(lengths, source)
    width = resp_rows.shape[2]
    rows_here = T_MB // seg_count
    tokens = MB * T_MB
    block = tokens // seg_count

    def ordered(table):
        return table.reshape(MB, seg_count, rows_here).transpose(1, 0, 2).reshape(-1)

    slots = ordered(member + R_MB * jnp.arange(MB, dtype=jnp.int32)[:, None])
    spots = ordered(position)
    pick = ordered(owners) * LMAX + spots
    code = slots * T_MB + spots
    cosine, sine_part = angles(spots)
    cosine = jnp.concatenate([cosine, cosine], axis=1)
    signed_sine = jnp.concatenate([-sine_part, sine_part], axis=1)
    kv_width = w_keyval.shape[-1]
    q_width = w_query.shape[-1]
    kv_lanes = HEAD_DIM
    keyval_w = w_keyval[0, 0].reshape(D, 2 * kv_width)
    keyval_w = jnp.pad(keyval_w, ((0, 0), (0, kv_lanes - 2 * kv_width)))
    in_width = q_width + kv_lanes
    rows_pool = resp_rows.shape[0] * LMAX
    vmem = pl.BlockSpec(memory_space=pltpu.VMEM)
    hbm = pl.BlockSpec(memory_space=pl.ANY)
    group = HEAD_DIM // kv_width
    dma = pltpu.SemaphoreType.DMA
    hidden, scores, other = pl.pallas_call(
        functools.partial(stack_kernel, mp_count, seg_count, kv_width),
        out_shape=(
            jax.ShapeDtypeStruct((block, width), bf16),
            jax.ShapeDtypeStruct((8, tokens), f32),
            jax.ShapeDtypeStruct((8, tokens), f32),
        ),
        in_specs=[hbm] + [vmem] * 6 + [hbm] * 3 + [vmem] * 2,
        out_specs=(vmem, vmem, vmem),
        scratch_shapes=[
            pltpu.VMEM((seg_count, rows_pool, width // 2), bf16),
            pltpu.VMEM((tokens, width), bf16),
            pltpu.VMEM((mp_count, tokens, width), bf16),
            pltpu.VMEM((mp_count, 16, width), bf16),
            pltpu.VMEM((mp_count, width, q_width), bf16),
            pltpu.VMEM((mp_count, width, kv_lanes), bf16),
            pltpu.VMEM((D, q_width), bf16),
            pltpu.VMEM((D, kv_lanes), bf16),
            pltpu.VMEM((mp_count * q_width, width), bf16),
            pltpu.VMEM((mp_count, tokens, in_width), bf16),
            pltpu.VMEM((mp_count, tokens, in_width), bf16),
            pltpu.VMEM((tokens, in_width), f32),
            pltpu.VMEM((group, tokens, kv_lanes), bf16),
            pltpu.VMEM((tokens, mp_count * q_width), bf16),
            pltpu.VMEM((tokens, width), bf16),
            pltpu.VMEM((block, width), bf16),
            pltpu.VMEM((mp_count, 8, tokens), f32),
            pltpu.VMEM((8, tokens), f32),
            pltpu.VMEM((8, tokens), f32),
            dma((4,)),
            dma((2, seg_count)),
            dma((2, mp_count)),
            dma((2, mp_count)),
            dma((2, mp_count)),
            dma((2, 2 * mp_count)),
            dma((2, 2 * mp_count)),
            dma((2, 2 * mp_count)),
            dma((2, group)),
            dma((2, mp_count)),
            dma((2, 2)),
            dma((2, seg_count)),
            dma((2, mp_count)),
            dma((2, seg_count)),
            dma((2, 1)),
        ],
        compiler_params=pltpu.CompilerParams(
            collective_id=0, has_side_effects=True, vmem_limit_bytes=58 * 1024 * 1024
        ),
    )(
        resp_rows.reshape(rows_pool, width),
        pick[:, None],
        code[:, None],
        code[None, :],
        cosine,
        signed_sine,
        jnp.broadcast_to(gains[0], (16, width)),
        w_query[0, 0],
        keyval_w,
        w_out[0, 0],
        final_gain,
        head,
    )

    def restored(row):
        return row.reshape(seg_count, MB, rows_here).transpose(1, 0, 2).reshape(MB, T_MB)

    scores, other = restored(scores[0]), restored(other[0])
    hidden = hidden.reshape(1, MB, rows_here, width)
    places = jnp.arange(T_MB, dtype=jnp.int32)
    last_pick = (places[None, None, :] == (seg_ends - 1)[:, :, None]).astype(f32)
    section_no = lax.axis_index("section")
    gap = jnp.where(section_no == 0, scores - other, other - scores)
    gap_slot = jnp.sum(last_pick * gap[:, None, :], axis=-1).reshape(-1)
    half_count = RESP // 2
    response_ids = section_no * half_count + jnp.arange(half_count, dtype=jnp.int32)
    matches = (source[None, :] == response_ids[:, None]).astype(f32)
    own_part = jnp.sum(matches * gap_slot[None, :], axis=1)
    return (hidden, scores[None], own_part)


def solution(mesh):
    in_specs = (
        P(("groups", "segment"), None, "mp"),
        P("groups", None),
        P("groups"),
        P("section", "segment", None, "mp"),
        P("section", "segment", None, None, "mp"),
        P("section", "segment", None, "mp"),
        P("section", "segment", "mp"),
        P("section", "mp"),
        P("section", "mp"),
    )
    out_specs = (
        P("section", "groups", "segment", "mp"),
        P("section", "groups", None),
        P(("groups", "section")),
    )
    return jax.shard_map(
        per_device, mesh=mesh, in_specs=in_specs, out_specs=out_specs, check_vma=False
    )
```

```python
import functools

import jax
import jax.numpy as jnp
from jax import lax
from jax.experimental import pallas as pl
from jax.experimental.pallas import tpu as pltpu
from jax.sharding import PartitionSpec as P

D = 4096
HEAD_DIM = 128
GROUP = 8
MB = 4
R_MB = 4
T_MB = 64
LMAX = 32
RESP = 16


epsilon = 1e-06
rope_base = 1000000.0


def slot_tables(lengths, source):
    seg_ends = jnp.cumsum(lengths, axis=1)
    seg_starts = seg_ends - lengths
    places = jnp.arange(T_MB, dtype=jnp.int32)
    member = jnp.sum((places[None, :, None] >= seg_ends[:, None, :]).astype(jnp.int32), axis=2)
    one_hot = (member[:, :, None] == jnp.arange(R_MB, dtype=jnp.int32)[None, None, :]).astype(
        jnp.int32
    )
    position = places[None, :] - jnp.sum(one_hot * seg_starts[:, None, :], axis=2)
    owners = jnp.sum(one_hot * source.reshape(MB, R_MB)[:, None, :], axis=2)
    return (member, position, owners, seg_ends)


def angles(position):
    inv_freqs = rope_base ** (-jnp.arange(0, HEAD_DIM // 2, dtype=jnp.float32) * 2.0 / HEAD_DIM)
    phases = position.astype(jnp.float32)[..., None] * inv_freqs
    return (jnp.cos(phases), jnp.sin(phases))


def spin(block, cosine, signed_sine):
    return block * cosine + pltpu.roll(block, HEAD_DIM // 2, 1) * signed_sine


def stack_kernel(
    mp_count,
    seg_count,
    kv_width,
    resp,
    pick,
    code_col,
    code_row,
    cosine,
    signed_sine,
    gain,
    w_query,
    w_keyval,
    w_out,
    final_gain,
    head,
    hidden,
    scores,
    other_scores,
    pool,
    x_own,
    x_all,
    gain_all,
    query_part,
    keyval_part,
    query_own,
    keyval_own,
    w_proj,
    part_out,
    part_in,
    acc,
    kv_all,
    key_rows,
    value_rows,
    att,
    y,
    y_in,
    stats,
    total,
    total_other,
    local_sem,
    pool_sem,
    gain_sem,
    half_sem,
    swap_sem,
    w_sem,
    share_sem,
    part_sem,
    kv_sem,
    att_sem,
    next_sem,
    block_sem,
    stats_sem,
    total_sem,
    other_sem,
):
    f32, bf16 = jnp.float32, jnp.bfloat16
    me = lax.axis_index("mp")
    seg = lax.axis_index("segment")
    core = lax.axis_index("section")
    team = lax.axis_index("groups")
    tokens, width = x_own.shape
    in_width = acc.shape[1]
    q_width = att.shape[1] // mp_count
    rows_pool = resp.shape[0]
    half = tokens // 2
    half_width = width // 2
    block = tokens // seg_count
    last = seg_count - 1
    group = HEAD_DIM // kv_width

    def peer(d):
        return lax.rem(me + d, mp_count)

    def source_of(d):
        return lax.rem(me + mp_count - d, mp_count)

    def remote(src, dst, sems, slot, **place):
        return pltpu.make_async_remote_copy(
            src_ref=src,
            dst_ref=dst,
            send_sem=sems.at[0, slot],
            recv_sem=sems.at[1, slot],
            device_id=place,
            device_id_type=pl.DeviceIdType.MESH,
        )

    barrier = pltpu.get_barrier_semaphore()
    for d in range(1, mp_count):
        pl.semaphore_signal(
            barrier, inc=1, device_id={"mp": peer(d)}, device_id_type=pl.DeviceIdType.MESH
        )
    for d in range(1, seg_count):
        pl.semaphore_signal(
            barrier,
            inc=1,
            device_id={"segment": lax.rem(seg + d, seg_count)},
            device_id_type=pl.DeviceIdType.MESH,
        )
    pl.semaphore_signal(
        barrier, inc=1, device_id={"section": 1 - core}, device_id_type=pl.DeviceIdType.MESH
    )
    pl.semaphore_signal(
        barrier, inc=1, device_id={"groups": 1 - team}, device_id_type=pl.DeviceIdType.MESH
    )
    proj_copy = pltpu.make_async_copy(w_out, w_proj, local_sem.at[0])
    proj_copy.start()
    pl.semaphore_wait(barrier, mp_count + seg_count)

    def rows_of(index):
        return pl.ds(pl.multiple_of(index * width, width), width)

    kv_lanes = in_width - q_width
    my_columns = pl.ds(pl.multiple_of(core * half_width, half_width), half_width)

    def rows_at(r):
        return pl.ds(r * half, half)

    def gain_copy(d):
        return remote(gain, gain_all.at[me], gain_sem, d, mp=peer(d))

    def shard_copy(r, d):
        return remote(
            x_own.at[rows_at(r), my_columns],
            x_all.at[me, rows_at(r), my_columns],
            half_sem,
            r * mp_count + d,
            mp=peer(d),
        )

    def swap_copy(r, d):
        here = x_own.at[rows_at(r), my_columns]
        if d > 0:
            here = x_all.at[source_of(d), rows_at(r), my_columns]
        return remote(here, here, swap_sem, r * mp_count + d, section=1 - core)

    def part_copy(r, d):
        mine = rows_at(r)
        return remote(
            part_out.at[d, mine], part_in.at[d, mine], part_sem, r * mp_count + d, mp=peer(d)
        )

    @pl.when(seg == 0)
    def _():
        own_rows = pltpu.make_async_copy(resp.at[:, my_columns], pool.at[0], local_sem.at[3])
        own_rows.start()
        own_query = pltpu.make_async_copy(w_query, query_own, local_sem.at[1])
        own_query.start()
        own_keyval = pltpu.make_async_copy(w_keyval, keyval_own, local_sem.at[2])
        own_keyval.start()
        gain_all[me] = gain[...]
        for d in range(1, mp_count):
            gain_copy(d).start()
        row_ids = lax.broadcasted_iota(jnp.int32, (tokens, rows_pool), 1)
        chosen = [
            (pick[...] - s * rows_pool == row_ids).astype(f32).astype(bf16) for s in range(seg_count)
        ]
        own_rows.wait()
        for s in range(1, seg_count):
            remote(resp.at[:, my_columns], pool.at[s], pool_sem, s, segment=0).wait_recv()
        step = min(256, half_width)
        for at in range(0, half_width, step):
            found = jnp.dot(chosen[0], pool[0, :, at : at + step], preferred_element_type=f32)
            for s in range(1, seg_count):
                found += jnp.dot(chosen[s], pool[s, :, at : at + step], preferred_element_type=f32)
            x_own[:, pl.ds(pl.multiple_of(core * half_width + at, step), step)] = found.astype(bf16)
        for r in range(2):
            for d in range(1, mp_count):
                shard_copy(r, d).start()
            swap_copy(r, 0).start()
        own_query.wait()
        own_keyval.wait()
        for d in range(1, mp_count):
            gain_copy(d).wait_recv()

    @pl.when(seg > 0)
    def _():
        rows_copy = remote(resp.at[:, my_columns], pool.at[seg], pool_sem, seg, segment=0)
        rows_copy.start()
        upper_rows = pl.ds(pl.multiple_of(team * half_width, half_width), half_width)
        weights = [(w_query, query_part), (w_keyval, keyval_part)]
        shards = []
        shares = []
        for i, (whole, part) in enumerate(weights):
            for d in range(1, mp_count):
                rows = pl.ds(
                    pl.multiple_of(peer(d) * width + team * half_width, half_width), half_width
                )
                here = part.at[source_of(d), upper_rows]
                slot = i * mp_count + d
                shards.append(
                    remote(whole.at[rows], part.at[me, upper_rows], w_sem, slot, mp=peer(d))
                )
                shares.append(remote(here, here, share_sem, slot, groups=1 - team))
        for copy in shards:
            copy.start()
        for i, (whole, part) in enumerate(weights):
            own = pltpu.make_async_copy(whole.at[rows_of(me)], part.at[me], local_sem.at[1 + i])
            own.start()
            own.wait()
        rows_copy.wait_send()
        for copy, share in zip(shards, shares):
            copy.wait_recv()
            share.start()
        for share in shares:
            share.wait()
        for copy in shards:
            copy.wait_send()

    slot = lax.rem(me, group)
    lane = lax.broadcasted_iota(jnp.int32, (half, kv_lanes), 1)
    head_count = q_width // HEAD_DIM
    att_columns = pl.ds(pl.multiple_of(me * q_width, q_width), q_width)
    order = []
    for d in range(1, mp_count // 2 + 1):
        order += [d] if 2 * d == mp_count else [d, mp_count - d]

    def project_in(r):
        mine = rows_at(r)

        @pl.when(seg == 0)
        def _():
            acc[mine] = jnp.zeros((half, in_width), f32)

            def add(d):
                swap_copy(r, d).wait_recv()
                if d == 0:
                    values, gains_row, index = x_own[mine], gain[0:1], me
                else:
                    index = source_of(d)
                    values, gains_row = x_all[index, mine], gain_all[index, 0:1]
                rows = values.astype(f32)
                squares = jnp.sum(rows * rows, axis=1, keepdims=True)
                lifted = (rows * gains_row.astype(f32)).astype(bf16)
                at = rows_of(index)
                acc[mine, :q_width] += jnp.dot(lifted, query_own[at], preferred_element_type=f32)
                keyval = jnp.dot(lifted, keyval_own[at], preferred_element_type=f32)
                acc[mine, q_width:] += keyval + jnp.where(lane == 2 * kv_width, squares, 0.0)

            done = 0
            for d in order:
                shard_copy(r, d).wait_recv()
                swap_copy(r, d).start()
                add(done)
                done = d
            add(done)

        @pl.when(seg > 0)
        def _():
            onward(r).wait_recv()
            rows = x_own[mine].astype(f32)
            squares = jnp.sum(rows * rows, axis=1, keepdims=True)
            upper = squares.astype(bf16).astype(f32)
            extra = jnp.where(
                lane == 2 * kv_width,
                upper,
                jnp.where(lane == 2 * kv_width + 1, squares - upper, 0.0),
            )
            lifted = (rows * gain[0:1].astype(f32)).astype(bf16)
            for d in range(1, mp_count):
                index = peer(d)
                part_out[d, mine, :q_width] = jnp.dot(
                    lifted, query_part[index], preferred_element_type=f32
                ).astype(bf16)
                part_out[d, mine, q_width:] = (
                    jnp.dot(lifted, keyval_part[index], preferred_element_type=f32) + extra
                ).astype(bf16)
                part_copy(r, d).start()
            acc[mine, :q_width] = jnp.dot(lifted, query_part[me], preferred_element_type=f32)
            acc[mine, q_width:] = (
                jnp.dot(lifted, keyval_part[me], preferred_element_type=f32) + extra
            )
            for d in order:
                part_copy(r, d).wait_recv()
                acc[mine] += part_in[d, mine].astype(f32)

    def att_copy(r, d):
        here = att.at[rows_at(r), att_columns]
        return remote(here, here, att_sem, r * mp_count + d, mp=peer(d))

    def attend(r):
        mine = rows_at(r)
        seen = (r + 1) * half
        ss_at = q_width + 2 * kv_width
        squares = acc[mine, ss_at : ss_at + 1] + acc[mine, ss_at + 1 : ss_at + 2]
        scale = lax.rsqrt(squares / D + epsilon)
        kv_all[slot, mine] = (acc[mine, q_width:] * scale).astype(bf16)
        kv_copies = [
            remote(
                kv_all.at[slot, mine],
                kv_all.at[slot, mine],
                kv_sem,
                r * group + d,
                mp=me - slot + lax.rem(slot + d, group),
            )
            for d in range(1, group)
        ]
        for copy in kv_copies:
            copy.start()
        cos_here, sin_here = cosine[mine], signed_sine[mine]
        queries = []
        for h in range(head_count):
            vectors = acc[mine, h * HEAD_DIM : (h + 1) * HEAD_DIM] * scale
            queries.append(spin(vectors, cos_here, sin_here).astype(bf16))
        codes = code_row[:, :seen]
        own_codes = code_col[mine]
        visible = (codes <= own_codes) & (codes >= own_codes // T_MB * T_MB)
        from_lane = lax.broadcasted_iota(jnp.int32, (kv_lanes, 2 * HEAD_DIM), 0)
        to_lane = lax.broadcasted_iota(jnp.int32, (kv_lanes, 2 * HEAD_DIM), 1)
        for copy in kv_copies:
            copy.wait()
        keyval = jnp.zeros((half, 2 * HEAD_DIM), f32)
        for g in range(group):
            place = jnp.where(
                from_lane < kv_width,
                from_lane + g * kv_width,
                from_lane - kv_width + HEAD_DIM + g * kv_width,
            )
            moved = (place == to_lane) & (from_lane < 2 * kv_width)
            keyval += jnp.dot(
                kv_all[g, mine], moved.astype(f32).astype(bf16), preferred_element_type=f32
            )
        key_rows[mine] = spin(keyval[:, :HEAD_DIM], cos_here, sin_here).astype(bf16)
        value_rows[mine] = keyval[:, HEAD_DIM:].astype(bf16)
        outs = []
        for h in range(head_count):
            logits = lax.dot_general(
                queries[h], key_rows[:seen], (((1,), (1,)), ((), ())), preferred_element_type=f32
            ) * HEAD_DIM ** (-0.5)
            logits = jnp.where(visible, logits, -1e30)
            expo = jnp.exp(logits - jnp.max(logits, axis=1, keepdims=True))
            weights = (expo / jnp.sum(expo, axis=1, keepdims=True)).astype(bf16)
            outs.append(
                jnp.dot(weights, value_rows[:seen], preferred_element_type=f32).astype(bf16)
            )
        att[mine, att_columns] = jnp.concatenate(outs, axis=1)
        for d in range(1, mp_count):
            att_copy(r, d).start()

    step = 256

    def onward(r):
        mine = pl.ds(r * half, half)
        return remote(
            y.at[mine], x_own.at[mine], next_sem, r, segment=lax.rem(seg + 1, seg_count)
        )

    def project_out(r):
        mine = rows_at(r)
        for d in range(1, mp_count):
            att_copy(r, d).wait()
        for at in range(0, width, step):
            projected = jnp.dot(
                att[mine], w_proj[:, at : at + step], preferred_element_type=f32
            )
            y[mine, at : at + step] = (
                x_own[mine, at : at + step].astype(f32) + projected
            ).astype(bf16)

        @pl.when(seg < last)
        def _():
            onward(r).start()

    project_in(0)
    attend(0)
    project_in(1)
    proj_copy.wait()
    project_out(0)
    attend(1)
    project_out(1)

    @pl.when(seg == 0)
    def _():
        for d in range(1, mp_count):
            gain_copy(d).wait_send()
        for r in range(2):
            for d in range(mp_count):
                swap_copy(r, d).wait_send()
                if d > 0:
                    shard_copy(r, d).wait_send()

    @pl.when(seg > 0)
    def _():
        for r in range(2):
            for d in range(1, mp_count):
                part_copy(r, d).wait_send()

    lift = final_gain[...].astype(f32)
    lift_head = lift * head[...].astype(f32)

    @pl.when(seg < last)
    def _():
        for r in range(2):
            onward(r).wait_send()
        remote(y.at[pl.ds(0, block)], y_in, block_sem, seg, segment=0).wait_recv()
        remote(total, total, total_sem, seg, segment=0).wait_recv()

    @pl.when(seg == last)
    def _():
        blocks = [
            remote(y.at[pl.ds(i * block, block)], y_in, block_sem, i, segment=i)
            for i in range(last)
        ]
        for copy in blocks:
            copy.start()
        rows = y[...].astype(f32)
        squares = jnp.sum(rows * rows, axis=1, keepdims=True)
        dots = jnp.sum(rows * lift_head, axis=1, keepdims=True)
        lane = lax.broadcasted_iota(jnp.int32, (tokens, HEAD_DIM), 1)
        both = jnp.where(lane == 0, squares, jnp.where(lane == 1, dots, 0.0))
        stats[0] = jnp.transpose(both)[:8]
        copies = [
            remote(stats.at[0], stats.at[d], stats_sem, d, mp=peer(d)) for d in range(1, mp_count)
        ]
        for copy in copies:
            copy.start()
        for copy in copies:
            copy.wait()
        total[...] = jnp.sum(stats[...], axis=0)
        totals = [remote(total, total, total_sem, i, segment=i) for i in range(last)]
        for copy in totals:
            copy.start()
        for copy in blocks + totals:
            copy.wait_send()
        y_in[...] = y[last * block : (last + 1) * block]

    swap = remote(total, total_other, other_sem, 0, section=1 - core)
    swap.start()
    row_scale = lax.rsqrt(total[0:1] / D + epsilon)
    scores[...] = jnp.broadcast_to(total[1:2] * row_scale, scores.shape)
    at_token = lax.broadcasted_iota(jnp.int32, (block, tokens), 1)
    wanted = lax.broadcasted_iota(jnp.int32, (block, tokens), 0) + seg * block
    column = jnp.sum(jnp.where(at_token == wanted, row_scale, 0.0), axis=1, keepdims=True)
    hidden[...] = (y_in[...].astype(f32) * column * lift).astype(bf16)
    swap.wait()
    other_scores[...] = jnp.broadcast_to(
        total_other[1:2] * lax.rsqrt(total_other[0:1] / D + epsilon), other_scores.shape
    )


def per_device(resp_rows, lengths, source, w_query, w_keyval, w_out, gains, final_gain, head):
    seg_count = lax.axis_size("segment")
    mp_count = lax.axis_size("mp")
    f32, bf16 = jnp.float32, jnp.bfloat16
    member, position, owners, seg_ends = slot_tables(lengths, source)
    width = resp_rows.shape[2]
    rows_here = T_MB // seg_count
    tokens = MB * T_MB
    block = tokens // seg_count

    def ordered(table):
        return table.reshape(MB, seg_count, rows_here).transpose(1, 0, 2).reshape(-1)

    slots = ordered(member + R_MB * jnp.arange(MB, dtype=jnp.int32)[:, None])
    spots = ordered(position)
    pick = ordered(owners) * LMAX + spots
    code = slots * T_MB + spots
    cosine, sine_part = angles(spots)
    cosine = jnp.concatenate([cosine, cosine], axis=1)
    signed_sine = jnp.concatenate([-sine_part, sine_part], axis=1)
    kv_width = w_keyval.shape[-1]
    q_width = w_query.shape[-1]
    kv_lanes = HEAD_DIM
    keyval_w = w_keyval[0, 0].reshape(D, 2 * kv_width)
    keyval_w = jnp.pad(keyval_w, ((0, 0), (0, kv_lanes - 2 * kv_width)))
    in_width = q_width + kv_lanes
    rows_pool = resp_rows.shape[0] * LMAX
    vmem = pl.BlockSpec(memory_space=pltpu.VMEM)
    hbm = pl.BlockSpec(memory_space=pl.ANY)
    group = HEAD_DIM // kv_width
    dma = pltpu.SemaphoreType.DMA
    hidden, scores, other = pl.pallas_call(
        functools.partial(stack_kernel, mp_count, seg_count, kv_width),
        out_shape=(
            jax.ShapeDtypeStruct((block, width), bf16),
            jax.ShapeDtypeStruct((8, tokens), f32),
            jax.ShapeDtypeStruct((8, tokens), f32),
        ),
        in_specs=[hbm] + [vmem] * 6 + [hbm] * 3 + [vmem] * 2,
        out_specs=(vmem, vmem, vmem),
        scratch_shapes=[
            pltpu.VMEM((seg_count, rows_pool, width // 2), bf16),
            pltpu.VMEM((tokens, width), bf16),
            pltpu.VMEM((mp_count, tokens, width), bf16),
            pltpu.VMEM((mp_count, 16, width), bf16),
            pltpu.VMEM((mp_count, width, q_width), bf16),
            pltpu.VMEM((mp_count, width, kv_lanes), bf16),
            pltpu.VMEM((D, q_width), bf16),
            pltpu.VMEM((D, kv_lanes), bf16),
            pltpu.VMEM((mp_count * q_width, width), bf16),
            pltpu.VMEM((mp_count, tokens, in_width), bf16),
            pltpu.VMEM((mp_count, tokens, in_width), bf16),
            pltpu.VMEM((tokens, in_width), f32),
            pltpu.VMEM((group, tokens, kv_lanes), bf16),
            pltpu.VMEM((tokens, HEAD_DIM), bf16),
            pltpu.VMEM((tokens, HEAD_DIM), bf16),
            pltpu.VMEM((tokens, mp_count * q_width), bf16),
            pltpu.VMEM((tokens, width), bf16),
            pltpu.VMEM((block, width), bf16),
            pltpu.VMEM((mp_count, 8, tokens), f32),
            pltpu.VMEM((8, tokens), f32),
            pltpu.VMEM((8, tokens), f32),
            dma((4,)),
            dma((2, seg_count)),
            dma((2, mp_count)),
            dma((2, 2 * mp_count)),
            dma((2, 2 * mp_count)),
            dma((2, 2 * mp_count)),
            dma((2, 2 * mp_count)),
            dma((2, 2 * mp_count)),
            dma((2, 2 * group)),
            dma((2, 2 * mp_count)),
            dma((2, 2)),
            dma((2, seg_count)),
            dma((2, mp_count)),
            dma((2, seg_count)),
            dma((2, 1)),
        ],
        compiler_params=pltpu.CompilerParams(
            collective_id=0, has_side_effects=True, vmem_limit_bytes=58 * 1024 * 1024
        ),
    )(
        resp_rows.reshape(rows_pool, width),
        pick[:, None],
        code[:, None],
        code[None, :],
        cosine,
        signed_sine,
        jnp.broadcast_to(gains[0], (16, width)),
        w_query[0, 0],
        keyval_w,
        w_out[0, 0],
        final_gain,
        head,
    )

    def restored(row):
        return row.reshape(seg_count, MB, rows_here).transpose(1, 0, 2).reshape(MB, T_MB)

    scores, other = restored(scores[0]), restored(other[0])
    hidden = hidden.reshape(1, MB, rows_here, width)
    places = jnp.arange(T_MB, dtype=jnp.int32)
    last_pick = (places[None, None, :] == (seg_ends - 1)[:, :, None]).astype(f32)
    section_no = lax.axis_index("section")
    gap = jnp.where(section_no == 0, scores - other, other - scores)
    gap_slot = jnp.sum(last_pick * gap[:, None, :], axis=-1).reshape(-1)
    half_count = RESP // 2
    response_ids = section_no * half_count + jnp.arange(half_count, dtype=jnp.int32)
    matches = (source[None, :] == response_ids[:, None]).astype(f32)
    own_part = jnp.sum(matches * gap_slot[None, :], axis=1)
    return (hidden, scores[None], own_part)


def solution(mesh):
    in_specs = (
        P(("groups", "segment"), None, "mp"),
        P("groups", None),
        P("groups"),
        P("section", "segment", None, "mp"),
        P("section", "segment", None, None, "mp"),
        P("section", "segment", None, "mp"),
        P("section", "segment", "mp"),
        P("section", "mp"),
        P("section", "mp"),
    )
    out_specs = (
        P("section", "groups", "segment", "mp"),
        P("section", "groups", None),
        P(("groups", "section")),
    )
    return jax.shard_map(
        per_device, mesh=mesh, in_specs=in_specs, out_specs=out_specs, check_vma=False
    )
```

```python
import functools

import jax
import jax.numpy as jnp
from jax import lax
from jax.experimental import pallas as pl
from jax.experimental.pallas import tpu as pltpu
from jax.sharding import PartitionSpec as P

D = 4096
HEAD_DIM = 128
GROUP = 8
MB = 4
R_MB = 4
T_MB = 64
LMAX = 32
RESP = 16


epsilon = 1e-06
rope_base = 1000000.0


def slot_tables(lengths, source):
    seg_ends = jnp.cumsum(lengths, axis=1)
    seg_starts = seg_ends - lengths
    places = jnp.arange(T_MB, dtype=jnp.int32)
    member = jnp.sum((places[None, :, None] >= seg_ends[:, None, :]).astype(jnp.int32), axis=2)
    one_hot = (member[:, :, None] == jnp.arange(R_MB, dtype=jnp.int32)[None, None, :]).astype(
        jnp.int32
    )
    position = places[None, :] - jnp.sum(one_hot * seg_starts[:, None, :], axis=2)
    owners = jnp.sum(one_hot * source.reshape(MB, R_MB)[:, None, :], axis=2)
    return (member, position, owners, seg_ends)


def angles(position):
    inv_freqs = rope_base ** (-jnp.arange(0, HEAD_DIM // 2, dtype=jnp.float32) * 2.0 / HEAD_DIM)
    phases = position.astype(jnp.float32)[..., None] * inv_freqs
    return (jnp.cos(phases), jnp.sin(phases))


def spin(block, cosine, signed_sine):
    return block * cosine + pltpu.roll(block, HEAD_DIM // 2, 1) * signed_sine


def stack_kernel(
    mp_count,
    seg_count,
    kv_width,
    resp,
    pick,
    code_col,
    code_row,
    cosine,
    signed_sine,
    gain,
    w_query,
    w_keyval,
    w_out,
    final_gain,
    head,
    hidden,
    scores,
    other_scores,
    pool,
    x_own,
    x_all,
    gain_all,
    query_part,
    keyval_part,
    query_own,
    keyval_own,
    w_proj,
    part_out,
    part_in,
    acc,
    kv_all,
    key_rows,
    value_rows,
    att,
    y,
    y_in,
    stats,
    total,
    total_other,
    local_sem,
    pool_sem,
    gain_sem,
    half_sem,
    swap_sem,
    w_sem,
    share_sem,
    part_sem,
    kv_sem,
    att_sem,
    next_sem,
    block_sem,
    stats_sem,
    total_sem,
    other_sem,
):
    f32, bf16 = jnp.float32, jnp.bfloat16
    me = lax.axis_index("mp")
    seg = lax.axis_index("segment")
    core = lax.axis_index("section")
    team = lax.axis_index("groups")
    tokens, width = x_own.shape
    in_width = acc.shape[1]
    q_width = att.shape[1] // mp_count
    rows_pool = resp.shape[0]
    half = tokens // 2
    half_width = width // 2
    block = tokens // seg_count
    last = seg_count - 1
    group = HEAD_DIM // kv_width

    def peer(d):
        return lax.rem(me + d, mp_count)

    def source_of(d):
        return lax.rem(me + mp_count - d, mp_count)

    def remote(src, dst, sems, slot, **place):
        return pltpu.make_async_remote_copy(
            src_ref=src,
            dst_ref=dst,
            send_sem=sems.at[0, slot],
            recv_sem=sems.at[1, slot],
            device_id=place,
            device_id_type=pl.DeviceIdType.MESH,
        )

    barrier = pltpu.get_barrier_semaphore()
    for d in range(1, mp_count):
        pl.semaphore_signal(
            barrier, inc=1, device_id={"mp": peer(d)}, device_id_type=pl.DeviceIdType.MESH
        )
    for d in range(1, seg_count):
        pl.semaphore_signal(
            barrier,
            inc=1,
            device_id={"segment": lax.rem(seg + d, seg_count)},
            device_id_type=pl.DeviceIdType.MESH,
        )
    pl.semaphore_signal(
        barrier, inc=1, device_id={"section": 1 - core}, device_id_type=pl.DeviceIdType.MESH
    )
    pl.semaphore_signal(
        barrier, inc=1, device_id={"groups": 1 - team}, device_id_type=pl.DeviceIdType.MESH
    )
    proj_copy = pltpu.make_async_copy(w_out, w_proj, local_sem.at[0])
    proj_copy.start()
    pl.semaphore_wait(barrier, mp_count + seg_count)

    def rows_of(index):
        return pl.ds(pl.multiple_of(index * width, width), width)

    kv_lanes = in_width - q_width
    my_columns = pl.ds(pl.multiple_of(core * half_width, half_width), half_width)

    def rows_at(r):
        return pl.ds(r * half, half)

    def gain_copy(d):
        return remote(gain, gain_all.at[me], gain_sem, d, mp=peer(d))

    def shard_copy(r, d):
        return remote(
            x_own.at[rows_at(r), my_columns],
            x_all.at[me, rows_at(r), my_columns],
            half_sem,
            r * mp_count + d,
            mp=peer(d),
        )

    def swap_copy(r, d):
        here = x_own.at[rows_at(r), my_columns]
        if d > 0:
            here = x_all.at[source_of(d), rows_at(r), my_columns]
        return remote(here, here, swap_sem, r * mp_count + d, section=1 - core)

    def part_copy(r, d):
        mine = rows_at(r)
        return remote(
            part_out.at[d, mine], part_in.at[d, mine], part_sem, r * mp_count + d, mp=peer(d)
        )

    @pl.when(seg == 0)
    def _():
        own_rows = pltpu.make_async_copy(resp.at[:, my_columns], pool.at[0], local_sem.at[3])
        own_rows.start()
        own_query = pltpu.make_async_copy(w_query, query_own, local_sem.at[1])
        own_query.start()
        own_keyval = pltpu.make_async_copy(w_keyval, keyval_own, local_sem.at[2])
        own_keyval.start()
        gain_all[me] = gain[...]
        for d in range(1, mp_count):
            gain_copy(d).start()
        row_ids = lax.broadcasted_iota(jnp.int32, (tokens, rows_pool), 1)
        chosen = [
            (pick[...] - s * rows_pool == row_ids).astype(f32).astype(bf16) for s in range(seg_count)
        ]
        own_rows.wait()
        for s in range(1, seg_count):
            remote(resp.at[:, my_columns], pool.at[s], pool_sem, s, segment=0).wait_recv()
        step = min(256, half_width)
        for at in range(0, half_width, step):
            found = jnp.dot(chosen[0], pool[0, :, at : at + step], preferred_element_type=f32)
            for s in range(1, seg_count):
                found += jnp.dot(chosen[s], pool[s, :, at : at + step], preferred_element_type=f32)
            x_own[:, pl.ds(pl.multiple_of(core * half_width + at, step), step)] = found.astype(bf16)
        for d in range(1, mp_count):
            shard_copy(0, d).start()
        for r in range(2):
            swap_copy(r, 0).start()
        own_query.wait()
        own_keyval.wait()
        for d in range(1, mp_count):
            gain_copy(d).wait_recv()

    @pl.when(seg > 0)
    def _():
        rows_copy = remote(resp.at[:, my_columns], pool.at[seg], pool_sem, seg, segment=0)
        rows_copy.start()
        upper_rows = pl.ds(pl.multiple_of(team * half_width, half_width), half_width)
        weights = [(w_query, query_part), (w_keyval, keyval_part)]
        shards = []
        shares = []
        for i, (whole, part) in enumerate(weights):
            for d in range(1, mp_count):
                rows = pl.ds(
                    pl.multiple_of(peer(d) * width + team * half_width, half_width), half_width
                )
                here = part.at[source_of(d), upper_rows]
                slot = i * mp_count + d
                shards.append(
                    remote(whole.at[rows], part.at[me, upper_rows], w_sem, slot, mp=peer(d))
                )
                shares.append(remote(here, here, share_sem, slot, groups=1 - team))
        for copy in shards:
            copy.start()
        for i, (whole, part) in enumerate(weights):
            own = pltpu.make_async_copy(whole.at[rows_of(me)], part.at[me], local_sem.at[1 + i])
            own.start()
            own.wait()
        rows_copy.wait_send()
        for copy, share in zip(shards, shares):
            copy.wait_recv()
            share.start()
        for share in shares:
            share.wait()
        for copy in shards:
            copy.wait_send()

    slot = lax.rem(me, group)
    lane = lax.broadcasted_iota(jnp.int32, (half, kv_lanes), 1)
    head_count = q_width // HEAD_DIM
    att_columns = pl.ds(pl.multiple_of(me * q_width, q_width), q_width)
    order = []
    for d in range(1, mp_count // 2 + 1):
        order += [d] if 2 * d == mp_count else [d, mp_count - d]

    def project_in(r):
        mine = rows_at(r)

        @pl.when(seg == 0)
        def _():
            acc[mine] = jnp.zeros((half, in_width), f32)

            def add(d):
                swap_copy(r, d).wait_recv()
                if d == 0:
                    values, gains_row, index = x_own[mine], gain[0:1], me
                else:
                    index = source_of(d)
                    values, gains_row = x_all[index, mine], gain_all[index, 0:1]
                rows = values.astype(f32)
                squares = jnp.sum(rows * rows, axis=1, keepdims=True)
                lifted = (rows * gains_row.astype(f32)).astype(bf16)
                at = rows_of(index)
                acc[mine, :q_width] += jnp.dot(lifted, query_own[at], preferred_element_type=f32)
                keyval = jnp.dot(lifted, keyval_own[at], preferred_element_type=f32)
                acc[mine, q_width:] += keyval + jnp.where(lane == 2 * kv_width, squares, 0.0)

            done = 0
            for d in order:
                shard_copy(r, d).wait_recv()
                swap_copy(r, d).start()
                if r == 0 and d == order[-1]:
                    for later in range(1, mp_count):
                        shard_copy(1, later).start()
                add(done)
                done = d
            add(done)

        @pl.when(seg > 0)
        def _():
            onward(r).wait_recv()
            rows = x_own[mine].astype(f32)
            squares = jnp.sum(rows * rows, axis=1, keepdims=True)
            upper = squares.astype(bf16).astype(f32)
            extra = jnp.where(
                lane == 2 * kv_width,
                upper,
                jnp.where(lane == 2 * kv_width + 1, squares - upper, 0.0),
            )
            lifted = (rows * gain[0:1].astype(f32)).astype(bf16)
            for d in range(1, mp_count):
                index = peer(d)
                part_out[d, mine, :q_width] = jnp.dot(
                    lifted, query_part[index], preferred_element_type=f32
                ).astype(bf16)
                part_out[d, mine, q_width:] = (
                    jnp.dot(lifted, keyval_part[index], preferred_element_type=f32) + extra
                ).astype(bf16)
                part_copy(r, d).start()
            acc[mine, :q_width] = jnp.dot(lifted, query_part[me], preferred_element_type=f32)
            acc[mine, q_width:] = (
                jnp.dot(lifted, keyval_part[me], preferred_element_type=f32) + extra
            )
            for d in order:
                part_copy(r, d).wait_recv()
                acc[mine] += part_in[d, mine].astype(f32)

    def att_copy(r, d):
        here = att.at[rows_at(r), att_columns]
        return remote(here, here, att_sem, r * mp_count + d, mp=peer(d))

    def attend(r):
        mine = rows_at(r)
        seen = (r + 1) * half
        ss_at = q_width + 2 * kv_width
        squares = acc[mine, ss_at : ss_at + 1] + acc[mine, ss_at + 1 : ss_at + 2]
        scale = lax.rsqrt(squares / D + epsilon)
        kv_all[slot, mine] = (acc[mine, q_width:] * scale).astype(bf16)
        kv_copies = [
            remote(
                kv_all.at[slot, mine],
                kv_all.at[slot, mine],
                kv_sem,
                r * group + d,
                mp=me - slot + lax.rem(slot + d, group),
            )
            for d in range(1, group)
        ]
        for copy in kv_copies:
            copy.start()
        cos_here, sin_here = cosine[mine], signed_sine[mine]
        queries = []
        for h in range(head_count):
            vectors = acc[mine, h * HEAD_DIM : (h + 1) * HEAD_DIM] * scale
            queries.append(spin(vectors, cos_here, sin_here).astype(bf16))
        codes = code_row[:, :seen]
        own_codes = code_col[mine]
        visible = (codes <= own_codes) & (codes >= own_codes // T_MB * T_MB)
        from_lane = lax.broadcasted_iota(jnp.int32, (kv_lanes, 2 * HEAD_DIM), 0)
        to_lane = lax.broadcasted_iota(jnp.int32, (kv_lanes, 2 * HEAD_DIM), 1)
        for copy in kv_copies:
            copy.wait()
        keyval = jnp.zeros((half, 2 * HEAD_DIM), f32)
        for g in range(group):
            place = jnp.where(
                from_lane < kv_width,
                from_lane + g * kv_width,
                from_lane - kv_width + HEAD_DIM + g * kv_width,
            )
            moved = (place == to_lane) & (from_lane < 2 * kv_width)
            keyval += jnp.dot(
                kv_all[g, mine], moved.astype(f32).astype(bf16), preferred_element_type=f32
            )
        key_rows[mine] = spin(keyval[:, :HEAD_DIM], cos_here, sin_here).astype(bf16)
        value_rows[mine] = keyval[:, HEAD_DIM:].astype(bf16)
        outs = []
        for h in range(head_count):
            logits = lax.dot_general(
                queries[h], key_rows[:seen], (((1,), (1,)), ((), ())), preferred_element_type=f32
            ) * HEAD_DIM ** (-0.5)
            logits = jnp.where(visible, logits, -1e30)
            expo = jnp.exp(logits - jnp.max(logits, axis=1, keepdims=True))
            weights = (expo / jnp.sum(expo, axis=1, keepdims=True)).astype(bf16)
            outs.append(
                jnp.dot(weights, value_rows[:seen], preferred_element_type=f32).astype(bf16)
            )
        att[mine, att_columns] = jnp.concatenate(outs, axis=1)
        for d in range(1, mp_count):
            att_copy(r, d).start()

    step = 256

    def onward(r):
        mine = pl.ds(r * half, half)
        return remote(
            y.at[mine], x_own.at[mine], next_sem, r, segment=lax.rem(seg + 1, seg_count)
        )

    def project_out(r):
        mine = rows_at(r)
        for d in range(1, mp_count):
            att_copy(r, d).wait()
        for at in range(0, width, step):
            projected = jnp.dot(
                att[mine], w_proj[:, at : at + step], preferred_element_type=f32
            )
            y[mine, at : at + step] = (
                x_own[mine, at : at + step].astype(f32) + projected
            ).astype(bf16)

        @pl.when(seg < last)
        def _():
            onward(r).start()

    project_in(0)
    attend(0)
    project_in(1)
    proj_copy.wait()
    project_out(0)
    attend(1)
    project_out(1)

    @pl.when(seg == 0)
    def _():
        for d in range(1, mp_count):
            gain_copy(d).wait_send()
        for r in range(2):
            for d in range(mp_count):
                swap_copy(r, d).wait_send()
                if d > 0:
                    shard_copy(r, d).wait_send()

    @pl.when(seg > 0)
    def _():
        for r in range(2):
            for d in range(1, mp_count):
                part_copy(r, d).wait_send()

    lift = final_gain[...].astype(f32)
    lift_head = lift * head[...].astype(f32)

    @pl.when(seg < last)
    def _():
        for r in range(2):
            onward(r).wait_send()
        remote(y.at[pl.ds(0, block)], y_in, block_sem, seg, segment=0).wait_recv()
        remote(total, total, total_sem, seg, segment=0).wait_recv()

    @pl.when(seg == last)
    def _():
        blocks = [
            remote(y.at[pl.ds(i * block, block)], y_in, block_sem, i, segment=i)
            for i in range(last)
        ]
        for copy in blocks:
            copy.start()
        rows = y[...].astype(f32)
        squares = jnp.sum(rows * rows, axis=1, keepdims=True)
        dots = jnp.sum(rows * lift_head, axis=1, keepdims=True)
        lane = lax.broadcasted_iota(jnp.int32, (tokens, HEAD_DIM), 1)
        both = jnp.where(lane == 0, squares, jnp.where(lane == 1, dots, 0.0))
        stats[0] = jnp.transpose(both)[:8]
        copies = [
            remote(stats.at[0], stats.at[d], stats_sem, d, mp=peer(d)) for d in range(1, mp_count)
        ]
        for copy in copies:
            copy.start()
        for copy in copies:
            copy.wait()
        total[...] = jnp.sum(stats[...], axis=0)
        totals = [remote(total, total, total_sem, i, segment=i) for i in range(last)]
        for copy in totals:
            copy.start()
        for copy in blocks + totals:
            copy.wait_send()
        y_in[...] = y[last * block : (last + 1) * block]

    swap = remote(total, total_other, other_sem, 0, section=1 - core)
    swap.start()
    row_scale = lax.rsqrt(total[0:1] / D + epsilon)
    scores[...] = jnp.broadcast_to(total[1:2] * row_scale, scores.shape)
    at_token = lax.broadcasted_iota(jnp.int32, (block, tokens), 1)
    wanted = lax.broadcasted_iota(jnp.int32, (block, tokens), 0) + seg * block
    column = jnp.sum(jnp.where(at_token == wanted, row_scale, 0.0), axis=1, keepdims=True)
    hidden[...] = (y_in[...].astype(f32) * column * lift).astype(bf16)
    swap.wait()
    other_scores[...] = jnp.broadcast_to(
        total_other[1:2] * lax.rsqrt(total_other[0:1] / D + epsilon), other_scores.shape
    )


def per_device(resp_rows, lengths, source, w_query, w_keyval, w_out, gains, final_gain, head):
    seg_count = lax.axis_size("segment")
    mp_count = lax.axis_size("mp")
    f32, bf16 = jnp.float32, jnp.bfloat16
    member, position, owners, seg_ends = slot_tables(lengths, source)
    width = resp_rows.shape[2]
    rows_here = T_MB // seg_count
    tokens = MB * T_MB
    block = tokens // seg_count

    def ordered(table):
        return table.reshape(MB, seg_count, rows_here).transpose(1, 0, 2).reshape(-1)

    slots = ordered(member + R_MB * jnp.arange(MB, dtype=jnp.int32)[:, None])
    spots = ordered(position)
    pick = ordered(owners) * LMAX + spots
    code = slots * T_MB + spots
    cosine, sine_part = angles(spots)
    cosine = jnp.concatenate([cosine, cosine], axis=1)
    signed_sine = jnp.concatenate([-sine_part, sine_part], axis=1)
    kv_width = w_keyval.shape[-1]
    q_width = w_query.shape[-1]
    kv_lanes = HEAD_DIM
    keyval_w = w_keyval[0, 0].reshape(D, 2 * kv_width)
    keyval_w = jnp.pad(keyval_w, ((0, 0), (0, kv_lanes - 2 * kv_width)))
    in_width = q_width + kv_lanes
    rows_pool = resp_rows.shape[0] * LMAX
    vmem = pl.BlockSpec(memory_space=pltpu.VMEM)
    hbm = pl.BlockSpec(memory_space=pl.ANY)
    group = HEAD_DIM // kv_width
    dma = pltpu.SemaphoreType.DMA
    hidden, scores, other = pl.pallas_call(
        functools.partial(stack_kernel, mp_count, seg_count, kv_width),
        out_shape=(
            jax.ShapeDtypeStruct((block, width), bf16),
            jax.ShapeDtypeStruct((8, tokens), f32),
            jax.ShapeDtypeStruct((8, tokens), f32),
        ),
        in_specs=[hbm] + [vmem] * 6 + [hbm] * 3 + [vmem] * 2,
        out_specs=(vmem, vmem, vmem),
        scratch_shapes=[
            pltpu.VMEM((seg_count, rows_pool, width // 2), bf16),
            pltpu.VMEM((tokens, width), bf16),
            pltpu.VMEM((mp_count, tokens, width), bf16),
            pltpu.VMEM((mp_count, 16, width), bf16),
            pltpu.VMEM((mp_count, width, q_width), bf16),
            pltpu.VMEM((mp_count, width, kv_lanes), bf16),
            pltpu.VMEM((D, q_width), bf16),
            pltpu.VMEM((D, kv_lanes), bf16),
            pltpu.VMEM((mp_count * q_width, width), bf16),
            pltpu.VMEM((mp_count, tokens, in_width), bf16),
            pltpu.VMEM((mp_count, tokens, in_width), bf16),
            pltpu.VMEM((tokens, in_width), f32),
            pltpu.VMEM((group, tokens, kv_lanes), bf16),
            pltpu.VMEM((tokens, HEAD_DIM), bf16),
            pltpu.VMEM((tokens, HEAD_DIM), bf16),
            pltpu.VMEM((tokens, mp_count * q_width), bf16),
            pltpu.VMEM((tokens, width), bf16),
            pltpu.VMEM((block, width), bf16),
            pltpu.VMEM((mp_count, 8, tokens), f32),
            pltpu.VMEM((8, tokens), f32),
            pltpu.VMEM((8, tokens), f32),
            dma((4,)),
            dma((2, seg_count)),
            dma((2, mp_count)),
            dma((2, 2 * mp_count)),
            dma((2, 2 * mp_count)),
            dma((2, 2 * mp_count)),
            dma((2, 2 * mp_count)),
            dma((2, 2 * mp_count)),
            dma((2, 2 * group)),
            dma((2, 2 * mp_count)),
            dma((2, 2)),
            dma((2, seg_count)),
            dma((2, mp_count)),
            dma((2, seg_count)),
            dma((2, 1)),
        ],
        compiler_params=pltpu.CompilerParams(
            collective_id=0, has_side_effects=True, vmem_limit_bytes=58 * 1024 * 1024
        ),
    )(
        resp_rows.reshape(rows_pool, width),
        pick[:, None],
        code[:, None],
        code[None, :],
        cosine,
        signed_sine,
        jnp.broadcast_to(gains[0], (16, width)),
        w_query[0, 0],
        keyval_w,
        w_out[0, 0],
        final_gain,
        head,
    )

    def restored(row):
        return row.reshape(seg_count, MB, rows_here).transpose(1, 0, 2).reshape(MB, T_MB)

    scores, other = restored(scores[0]), restored(other[0])
    hidden = hidden.reshape(1, MB, rows_here, width)
    places = jnp.arange(T_MB, dtype=jnp.int32)
    last_pick = (places[None, None, :] == (seg_ends - 1)[:, :, None]).astype(f32)
    section_no = lax.axis_index("section")
    gap = jnp.where(section_no == 0, scores - other, other - scores)
    gap_slot = jnp.sum(last_pick * gap[:, None, :], axis=-1).reshape(-1)
    half_count = RESP // 2
    response_ids = section_no * half_count + jnp.arange(half_count, dtype=jnp.int32)
    matches = (source[None, :] == response_ids[:, None]).astype(f32)
    own_part = jnp.sum(matches * gap_slot[None, :], axis=1)
    return (hidden, scores[None], own_part)


def solution(mesh):
    in_specs = (
        P(("groups", "segment"), None, "mp"),
        P("groups", None),
        P("groups"),
        P("section", "segment", None, "mp"),
        P("section", "segment", None, None, "mp"),
        P("section", "segment", None, "mp"),
        P("section", "segment", "mp"),
        P("section", "mp"),
        P("section", "mp"),
    )
    out_specs = (
        P("section", "groups", "segment", "mp"),
        P("section", "groups", None),
        P(("groups", "section")),
    )
    return jax.shard_map(
        per_device, mesh=mesh, in_specs=in_specs, out_specs=out_specs, check_vma=False
    )
```
